256 devices in a mesh: tm: 4 (over x), space: 64 (over z, y, core).
Axes of the slice: x: 4, y: 4, z: 8, core: 2. Of those that a mesh axis runs over, the one named last changes fastest.
Arguments:
- init_state: float32 [64, 24576], P(None, 'space'), may hold values from -6 to 6
- guess: float32 [8, 64, 24576], P('tm', None, 'space'), may hold values from -6 to 6
- forcing: float32 [32, 64, 24576], P('tm', None, 'space'), may hold values from -3.5 to 3.5
- volume_block: float32 [64, 64], replicated
- face_blocks: float32 [3, 64, 64], replicated
- elem_scales: float32 [24576], P('space'), may hold values from 0.5 to 1.5
- element_ids: int32 [24576], P('space'), may hold values from 0 to 24575, as said below
- neighbours: int32 [6, 24576], P(None, 'space'), may hold values from 0 to 24575, as said below
- walls: int32 [6, 24576], P(None, 'space'), may hold values from 0 to 1, as said below
Outputs:
- corrected: float32 [8, 64, 24576], P('tm', None, 'space')
The draws below stay inside these ranges and needn't reach their ends.
Inputs may be any that keep to these rules, and one draw needn't show every extreme that they name: `element_ids`: the device at position d along space holds the elements d * 384 to (d + 1) * 384 - 1, each once, in a drawn order; element number ((z * 8) + y) * 8 + x sits at cell (x, y, z) of the grid. `neighbours`: faces in the order +x, -x, +y, -y, +z, -z; the grid is periodic in x and y; across the two end faces of the third dimension the neighbour is the element itself; a neighbour of an element held on a device is held by that device or is among the 64 lowest numbers of the next device or the 64 highest numbers of the previous one. `walls`: the end faces of the third dimension are closed, and a drawn set of interior faces; a face is closed from both of its sides.
All inputs are finite; a program needn't handle non-finite values.
Results may differ from the reference program's by a relative error of at most 0.0001.
Values sent between devices are 32-bit elements; how exact they have to be, the bound alone decides.
A program may use at most 64 MiB of HBM per device.

```python
import math
import jax
import jax.numpy as jnp
from jax import lax

DOF = 64
GX = 8
GY = 8
COARSEN = 4
E_DEV = 384
ELEMS = 24576
CPOINTS = 8
STEPS = 32


def grid_layout(key):
    devices = ELEMS // E_DEV
    keys = jax.random.split(key, devices)
    perms = jax.vmap(lambda one: jax.random.permutation(one, E_DEV))(keys)
    return (perms + (jnp.arange(devices, dtype=jnp.int32) * E_DEV)[:, None]).reshape(-1).astype(jnp.int32)


def closed_faces(key):
    return (jax.random.randint(jax.random.fold_in(key, 91), (3, ELEMS), 0, 8) == 0).astype(jnp.int32)


def neighbour_table(ids):
    layer = GX * GY
    depth = ELEMS // layer
    xpos = ids % GX
    ypos = ids // GX % GY
    zpos = ids // layer

    def number(xval, yval, zval):
        return (zval * GY + yval) * GX + xval
    upper = jnp.where(zpos == depth - 1, ids, number(xpos, ypos, zpos + 1))
    lower = jnp.where(zpos == 0, ids, number(xpos, ypos, zpos - 1))
    return jnp.stack([number((xpos + 1) % GX, ypos, zpos), number((xpos - 1) % GX, ypos, zpos), number(xpos, (ypos + 1) % GY, zpos), number(xpos, (ypos - 1) % GY, zpos), upper, lower]).astype(jnp.int32)


def draw_element_ids(key, part):
    ids = grid_layout(key)
    return ids


def draw_neighbours(key, part):
    ids = grid_layout(key)
    return neighbour_table(ids)


def draw_walls(key, part):
    ids = grid_layout(key)
    closed = closed_faces(key)
    table = neighbour_table(ids)
    depth = ELEMS // (GX * GY)
    zpos = ids // (GX * GY)
    top = (zpos == depth - 1).astype(jnp.int32)
    bottom = (zpos == 0).astype(jnp.int32)
    flags = jnp.stack([closed[0, ids], closed[0, table[1]], closed[1, ids], closed[1, table[3]], jnp.maximum(closed[2, ids], top), jnp.maximum(closed[2, table[5]], bottom)])
    return flags.astype(jnp.int32)


def draw_volume_block(key, part):
    key = jax.random.fold_in(key, 5)
    rate_key, skew_key = jax.random.split(key)
    rates = jnp.exp(jax.random.uniform(rate_key, (DOF,), jnp.float32, math.log(0.01), math.log(0.15)))
    raw = 0.007 * jax.random.normal(skew_key, (DOF, DOF), jnp.float32)
    return (raw - raw.T - jnp.diag(rates)).astype(jnp.float32)


def draw_face_blocks(key, part):
    key = jax.random.fold_in(key, 7)
    spread = jnp.array([0.005, 0.005, 0.02], jnp.float32)[:, None, None]
    raw = jax.random.normal(key, (3, DOF, DOF), jnp.float32)
    return (spread * raw).astype(jnp.float32)


def levels(rng, shape, cuts, least, top_value):
    factor_of = 1.0
    for dim, blocks in cuts:
        draws = jax.random.uniform(jax.random.fold_in(jax.random.fold_in(rng, 6), dim), (blocks,), jnp.float32, least / len(cuts), top_value / len(cuts))
        factor_of = factor_of * jnp.repeat(jnp.exp(draws), shape[dim] // blocks).reshape((-1,) + (1,) * (len(shape) - 1 - dim))
    return factor_of


def gaussian(own_key, extent, width, bound, cuts=(), kind=jnp.bfloat16):
    values = jax.random.normal(own_key, extent, jnp.float32) * width
    if len(cuts) > 0:
        values = levels(own_key, extent, cuts, -0.22, 0.18) * values
    return jnp.clip(values, min=-bound, max=bound).astype(kind)


def setup_inputs(seed: int = 0) -> dict:
    streams_of = jax.random.split(jax.random.key(seed), 10)
    return {
        "init_state": gaussian(streams_of[0], (DOF, ELEMS), 1.0, 6.0, ((1, 64),), jnp.float32),
        "guess": gaussian(streams_of[1], (CPOINTS, DOF, ELEMS), 1.0, 6.0, ((0, 4), (2, 64)), jnp.float32),
        "forcing": gaussian(streams_of[2], (STEPS, DOF, ELEMS), 0.6, 3.5, ((0, 4), (2, 64)), jnp.float32),
        "volume_block": draw_volume_block(jax.random.fold_in(streams_of[9], 71), 0),
        "face_blocks": draw_face_blocks(jax.random.fold_in(streams_of[9], 71), 0),
        "elem_scales": jnp.clip(jnp.exp(math.log(1.5) - 1.0986123 * jax.random.uniform(streams_of[5], (ELEMS,), jnp.float32) ** levels(streams_of[5], (ELEMS,), ((0, 64),), -0.2, 0.2)), 0.5, 1.5),
        "element_ids": draw_element_ids(jax.random.fold_in(streams_of[9], 71), 0),
        "neighbours": draw_neighbours(jax.random.fold_in(streams_of[9], 71), 0),
        "walls": draw_walls(jax.random.fold_in(streams_of[9], 71), 0),
    }


def make_blocks(face_blocks):
    parts = []
    for m in range(3):
        parts.append(face_blocks[m])
        parts.append(-face_blocks[m].T)
    return jnp.stack(parts)


def operate(state, volume_block, blocks, elem_scales, slot_of, open_mask):
    own = jnp.einsum('ij,cjn->cin', volume_block, state, precision=lax.Precision.HIGHEST) * elem_scales
    near = jnp.take(state, slot_of, axis=2) * open_mask
    return own + jnp.einsum('fij,cjfn->cin', blocks, near, precision=lax.Precision.HIGHEST)


def rk_step(state, size, apply_op):
    first = size * apply_op(state)
    second = size * apply_op(state + 0.5 * first)
    third = size * apply_op(state + 0.5 * second)
    fourth = size * apply_op(state + third)
    return state + (first + 2.0 * second + 2.0 * third + fourth) / 6.0


def reference(init_state, guess, forcing, volume_block, face_blocks, elem_scales, element_ids, neighbours, walls):
    blocks = make_blocks(face_blocks)
    inverse = jnp.zeros((ELEMS,), jnp.int32).at[element_ids].set(jnp.arange(ELEMS, dtype=jnp.int32))
    slot_of = inverse[neighbours]
    open_mask = (1 - walls).astype(jnp.float32)

    def apply_op(state):
        return operate(state, volume_block, blocks, elem_scales, slot_of, open_mask)

    starts = jnp.concatenate([init_state[None], guess[:-1]], axis=0)
    sources = forcing.reshape(CPOINTS, COARSEN, DOF, ELEMS)
    current = starts
    for inner in range(COARSEN):
        current = rk_step(current, 1.0, apply_op) + sources[:, inner]
    residual = current - guess

    def coarse(carry, term):
        carry = rk_step(carry, float(COARSEN), apply_op) + term
        return carry, carry[0]

    start = jnp.zeros_like(residual[:1])
    final, errors = lax.scan(coarse, start, residual[:, None])
    return guess + errors
```

```python
import functools
import jax
import jax.numpy as jnp
from jax import lax
from jax.experimental import pallas as pl
from jax.experimental.pallas import tpu as pltpu
from jax.sharding import PartitionSpec as P

GX = 8
LAYER = 64
DOF = 64
COARSEN = 4
HALO = 4
MESH = pl.DeviceIdType.MESH
F32 = jnp.float32
BF16 = jnp.bfloat16


def halves(x):
    hi = x.astype(BF16)
    return hi, (x - hi.astype(F32)).astype(BF16)


def thirds(x):
    hi = x.astype(BF16)
    rest = x - hi.astype(F32)
    mid = rest.astype(BF16)
    return hi, mid, (rest - mid.astype(F32)).astype(BF16)


def times_t(a, b):
    return lax.dot_general(a, b, (((1,), (1,)), ((), ())), preferred_element_type=F32)


def select_rows(perm, values):
    hi, mid, lo = thirds(values)
    return (times_t(perm, hi) + times_t(perm, mid)) + times_t(perm, lo)


def left_lanes(rows):
    return lax.broadcasted_iota(jnp.int32, (rows, 2 * DOF), 1) < DOF


def swapped(x):
    return pltpu.roll(x, DOF, 1)


def doubled(packed):
    left = left_lanes(packed.shape[0])
    other = swapped(packed)
    return jnp.where(left, packed, other), jnp.where(left, other, packed)


def one_hot(ids_row, first, rows):
    cells = lax.broadcasted_iota(jnp.int32, (rows, ids_row.shape[1]), 0) + first
    return (ids_row == cells).astype(F32).astype(BF16)


def table_of(perm, faces):
    flags = jnp.concatenate(
        [jnp.broadcast_to(faces[f : f + 1], (DOF, faces.shape[1])) for f in range(6)], axis=0
    )
    scale = jnp.broadcast_to(faces[6:7], (2 * DOF, faces.shape[1]))
    return times_t(perm, flags.astype(BF16)), select_rows(perm, scale)


def kernel(
    layers,
    count,
    init_ref,
    guess_ref,
    forcing_ref,
    volume_ref,
    faces_ref,
    scales_ref,
    ids_ref,
    walls_ref,
    out_ref,
    weights,
    table,
    perm_ref,
    sources,
    guess_grid,
    state,
    ext_a,
    ext_b,
    split_a,
    split_b,
    prod_a,
    prod_b,
    errors,
    faces_out,
    faces_in,
    guess_in,
    fine_out,
    fine_in,
    coarse_out,
    coarse_in,
    res_in,
    faces_send,
    faces_recv,
    guess_send,
    guess_recv,
    fine_send,
    fine_recv,
    coarse_send,
    coarse_recv,
    res_send,
    res_recv,
):
    times = lax.axis_size("tm")
    spaces = lax.axis_size("space")
    tme = lax.axis_index("tm")
    sme = lax.axis_index("space")
    up = lax.rem(sme + 1, spaces)
    down = lax.rem(sme + spaces - 1, spaces)
    own = layers * LAYER
    ext = layers + 2 * HALO

    barrier = pltpu.get_barrier_semaphore()
    pl.semaphore_signal(barrier, inc=1, device_id=(tme, up), device_id_type=MESH)
    pl.semaphore_signal(barrier, inc=1, device_id=(tme, down), device_id_type=MESH)
    for step in range(1, times):
        pl.semaphore_signal(
            barrier, inc=1, device_id=(lax.rem(tme + step, times), sme), device_id_type=MESH
        )

    local = ids_ref[...] - sme * own
    faces_out[0:6, :] = (1 - walls_ref[...]).astype(F32)
    faces_out[6:7, :] = scales_ref[...]
    faces_out[7:8, :] = local.astype(F32)

    pl.semaphore_wait(barrier, 2 + times - 1)

    def sends(source_up, source_down, target, send, recv):
        return (
            pltpu.make_async_remote_copy(
                src_ref=source_up,
                dst_ref=target(0),
                send_sem=send(0),
                recv_sem=recv(0),
                device_id=(tme, up),
                device_id_type=MESH,
            ),
            pltpu.make_async_remote_copy(
                src_ref=source_down,
                dst_ref=target(1),
                send_sem=send(1),
                recv_sem=recv(1),
                device_id=(tme, down),
                device_id_type=MESH,
            ),
        )

    guess_copy = pltpu.make_async_remote_copy(
        src_ref=guess_ref.at[count - 1],
        dst_ref=guess_in,
        send_sem=guess_send,
        recv_sem=guess_recv,
        device_id=(lax.rem(tme + 1, times), sme),
        device_id_type=MESH,
    )
    guess_copy.start()
    faces_copies = sends(
        faces_out,
        faces_out,
        lambda i: faces_in.at[i],
        lambda i: faces_send.at[i],
        lambda i: faces_recv.at[i],
    )
    for copy in faces_copies:
        copy.start()

    perm = one_hot(local, 0, own)
    perm_ref[...] = perm
    guess_grid[...] = select_rows(
        perm, jnp.concatenate([guess_ref[0], guess_ref[1]], axis=0)
    )
    blocks = []
    for m in range(3):
        face = faces_ref[m]
        blocks.append(face.T)
        blocks.append(-face)
    blocks.append(volume_ref[...].T)
    blocks.append(jnp.zeros((DOF, DOF), F32))
    for pair in range(4):
        high, low = halves(jnp.concatenate(blocks[2 * pair : 2 * pair + 2], axis=1))
        weights[:, pair * 2 * DOF : (pair + 1) * 2 * DOF] = jnp.concatenate(
            [high, high, low, low], axis=0
        )
    inner_flags, inner_scale = table_of(perm, faces_out[...])
    table[3 * LAYER : 3 * LAYER + own, 0 : 6 * DOF] = inner_flags
    table[3 * LAYER : 3 * LAYER + own, 6 * DOF : 8 * DOF] = inner_scale

    guess_copy.wait()
    first = jnp.where(tme == 0, init_ref[...], guess_in[...])
    state[...] = select_rows(perm, jnp.concatenate([first, guess_ref[0]], axis=0))

    def product(split, prod, low, high):
        rows = split[low * LAYER : high * LAYER, :]
        wide = jnp.concatenate([rows, rows], axis=1)
        prod[low * LAYER : high * LAYER, 4 * DOF :] = jnp.dot(
            wide, weights[:, 4 * DOF :], preferred_element_type=F32
        )
        prod[(low + 1) * LAYER : (high - 1) * LAYER, : 4 * DOF] = jnp.dot(
            wide[LAYER:-LAYER], weights[:, : 4 * DOF], preferred_element_type=F32
        )

    def combined(prod, layer):
        base = layer * LAYER
        left = left_lanes(LAYER)
        left3 = left.reshape(LAYER // GX, GX, 2 * DOF)
        px = prod[base : base + LAYER, 0 : 2 * DOF].reshape(LAYER // GX, GX, 2 * DOF)
        xs = jnp.where(left3, pltpu.roll(px, GX - 1, 1), pltpu.roll(px, 1, 1))
        py = prod[base : base + LAYER, 2 * DOF : 4 * DOF].reshape(LAYER // GX, GX, 2 * DOF)
        ys = jnp.where(
            left3,
            jnp.concatenate([py[1:], py[:1]], axis=0),
            jnp.concatenate([py[-1:], py[:-1]], axis=0),
        )
        zs = jnp.where(
            left,
            prod[base + LAYER : base + 2 * LAYER, 4 * DOF : 6 * DOF],
            prod[base - LAYER : base, 4 * DOF : 6 * DOF],
        )
        own_term = prod[base : base + LAYER, 6 * DOF : 8 * DOF]
        tb = base - LAYER
        total = (
            table[tb : tb + LAYER, 0 : 2 * DOF] * xs.reshape(LAYER, 2 * DOF)
            + table[tb : tb + LAYER, 2 * DOF : 4 * DOF] * ys.reshape(LAYER, 2 * DOF)
        ) + (
            table[tb : tb + LAYER, 4 * DOF : 6 * DOF] * zs
            + table[tb : tb + LAYER, 6 * DOF : 8 * DOF] * own_term
        )
        return total + swapped(total)

    def store_split(split, layer, value):
        low = value - value.astype(BF16).astype(F32)
        split[layer * LAYER : (layer + 1) * LAYER, :] = jnp.where(
            left_lanes(LAYER), value, low
        ).astype(BF16)

    def rk_steps(fields, size, finish):
        for x, split, prod in fields:
            for layer in range(ext):
                store_split(split, layer, x[layer * LAYER : (layer + 1) * LAYER, :])
        for stage in range(4):
            low, high = stage, ext - stage
            factor = size / (4 - stage)
            for x, split, prod in fields:
                product(split, prod, low, high)
            for index, (x, split, prod) in enumerate(fields):
                for layer in range(low + 1, high - 1):
                    value = x[layer * LAYER : (layer + 1) * LAYER, :] + factor * combined(prod, layer)
                    if stage < 3:
                        store_split(split, layer, value)
                    else:
                        finish(index, layer - HALO, value)

    def fine(inner, carry):
        parity = lax.rem(inner, 2)
        fine_out[...] = state[...]
        copies = sends(
            fine_out.at[pl.ds(own - HALO * LAYER, HALO * LAYER)],
            fine_out.at[pl.ds(0, HALO * LAYER)],
            lambda i: fine_in.at[parity, i],
            lambda i: fine_send.at[i],
            lambda i: fine_recv.at[parity, i],
        )
        for copy in copies:
            copy.start()

        @pl.when(inner == 0)
        def _():
            for step in range(COARSEN):
                pieces = jnp.concatenate([forcing_ref[step], forcing_ref[COARSEN + step]], axis=0)
                sources[step] = select_rows(perm_ref[...], pieces)
            for copy in faces_copies:
                copy.wait()
            for side in range(2):
                faces = faces_in[side]
                begin = own - 3 * LAYER if side == 0 else 0
                place = 0 if side == 0 else 3 * LAYER + own
                other = one_hot(faces[7:8].astype(jnp.int32), begin, 3 * LAYER)
                flags, scale = table_of(other, faces)
                table[place : place + 3 * LAYER, 0 : 6 * DOF] = flags
                table[place : place + 3 * LAYER, 6 * DOF : 8 * DOF] = scale

        def spread(layer, packed):
            one, two = doubled(packed)
            ext_a[layer * LAYER : (layer + 1) * LAYER, :] = one
            ext_b[layer * LAYER : (layer + 1) * LAYER, :] = two

        for layer in range(layers):
            spread(HALO + layer, state[layer * LAYER : (layer + 1) * LAYER, :])
        for copy in copies:
            copy.wait()
        for layer in range(HALO):
            rows = pl.ds(layer * LAYER, LAYER)
            spread(layer, fine_in[parity, 0, rows, :])
            spread(HALO + layers + layer, fine_in[parity, 1, rows, :])

        def finish(index, layer, value):
            rows = pl.ds(layer * LAYER, LAYER)
            if index == 0:
                state[rows, :] = value
            else:
                state[rows, :] = jnp.where(left_lanes(LAYER), state[rows, :], value) + sources[inner, rows, :]

        rk_steps(((ext_a, split_a, prod_a), (ext_b, split_b, prod_b)), 1.0, finish)
        return carry

    lax.fori_loop(0, COARSEN, fine, 0)

    res_in[tme] = state[...] - guess_grid[...]
    res_copies = []
    for step in range(1, times):
        target = lax.rem(tme + step, times)
        res_copies.append(
            pltpu.make_async_remote_copy(
                src_ref=res_in.at[tme],
                dst_ref=res_in.at[tme],
                send_sem=res_send.at[step],
                recv_sem=res_recv.at[step],
                device_id=(target, sme),
                device_id_type=MESH,
            )
        )
    for copy in res_copies:
        copy.start()
    for copy in res_copies:
        copy.wait()

    points = times * count
    for block in range(times):
        one, two = doubled(res_in[block])
        errors[2 * block] = one
        errors[2 * block + 1] = two

    def coarse(point, carry):
        parity = lax.rem(point, 2)
        half = HALO // 2
        for layer in range(half):
            rows = pl.ds(layer * LAYER, LAYER)
            left = left_lanes(LAYER)
            top = (layers - HALO + layer) * LAYER
            coarse_out[0, rows, :] = jnp.where(
                left,
                errors[point - 1, pl.ds(top, LAYER), :],
                errors[point - 1, pl.ds(top + half * LAYER, LAYER), :],
            )
            coarse_out[1, rows, :] = jnp.where(
                left,
                errors[point - 1, pl.ds(layer * LAYER, LAYER), :],
                errors[point - 1, pl.ds((layer + half) * LAYER, LAYER), :],
            )
        copies = sends(
            coarse_out.at[0],
            coarse_out.at[1],
            lambda i: coarse_in.at[parity, i],
            lambda i: coarse_send.at[i],
            lambda i: coarse_recv.at[parity, i],
        )
        for copy in copies:
            copy.start()
        ext_a[HALO * LAYER : HALO * LAYER + own, :] = errors[point - 1]
        for copy in copies:
            copy.wait()
        for side in range(2):
            base = 0 if side == 0 else HALO + layers
            for layer in range(half):
                one, two = doubled(coarse_in[parity, side, pl.ds(layer * LAYER, LAYER), :])
                ext_a[pl.ds((base + layer) * LAYER, LAYER), :] = one
                ext_a[pl.ds((base + half + layer) * LAYER, LAYER), :] = two

        def finish(index, layer, value):
            rows = pl.ds(layer * LAYER, LAYER)
            errors[point, rows, :] = errors[point, rows, :] + value

        rk_steps(((ext_a, split_a, prod_a),), float(COARSEN), finish)
        return carry

    lax.fori_loop(1, points, coarse, 0)

    packed = jnp.where(left_lanes(own), errors[count * tme], errors[count * tme + 1])
    parts = [
        lax.dot_general(part, perm_ref[...], (((0,), (0,)), ((), ())), preferred_element_type=F32)
        for part in thirds(packed)
    ]
    result = (parts[0] + parts[1]) + parts[2]
    out_ref[0] = result[:DOF]
    out_ref[1] = result[DOF:]


def body(init_state, guess, forcing, volume_block, face_blocks, elem_scales, element_ids, neighbours, walls):
    own = element_ids.shape[0]
    layers = own // LAYER
    count = guess.shape[0]
    times = lax.axis_size("tm")
    ext = (layers + 2 * HALO) * LAYER
    wide = 2 * DOF
    vmem = pl.BlockSpec(memory_space=pltpu.VMEM)
    dma = pltpu.SemaphoreType.DMA
    errors = pl.pallas_call(
        functools.partial(kernel, layers, count),
        out_shape=jax.ShapeDtypeStruct(guess.shape, F32),
        in_specs=[vmem] * 8,
        out_specs=vmem,
        scratch_shapes=[
            pltpu.VMEM((4 * DOF, 8 * DOF), BF16),
            pltpu.VMEM((own + 6 * LAYER, 8 * DOF), F32),
            pltpu.VMEM((own, own), BF16),
            pltpu.VMEM((COARSEN, own, wide), F32),
            pltpu.VMEM((own, wide), F32),
            pltpu.VMEM((own, wide), F32),
            pltpu.VMEM((ext, wide), F32),
            pltpu.VMEM((ext, wide), F32),
            pltpu.VMEM((ext, wide), BF16),
            pltpu.VMEM((ext, wide), BF16),
            pltpu.VMEM((ext, 8 * DOF), F32),
            pltpu.VMEM((ext, 8 * DOF), F32),
            pltpu.VMEM((times * count, own, wide), F32),
            pltpu.VMEM((8, own), F32),
            pltpu.VMEM((2, 8, own), F32),
            pltpu.VMEM((DOF, own), F32),
            pltpu.VMEM((own, wide), F32),
            pltpu.VMEM((2, 2, HALO * LAYER, wide), F32),
            pltpu.VMEM((2, HALO // 2 * LAYER, wide), F32),
            pltpu.VMEM((2, 2, HALO // 2 * LAYER, wide), F32),
            pltpu.VMEM((times, own, wide), F32),
            dma((2,)),
            dma((2,)),
            dma,
            dma,
            dma((2,)),
            dma((2, 2)),
            dma((2,)),
            dma((2, 2)),
            dma((times,)),
            dma((times,)),
        ],
        compiler_params=pltpu.CompilerParams(
            collective_id=0, has_side_effects=True, vmem_limit_bytes=48 * 1024 * 1024
        ),
    )(
        init_state,
        guess,
        forcing,
        volume_block,
        face_blocks,
        elem_scales.reshape(1, own),
        element_ids.reshape(1, own),
        walls,
    )
    return guess + errors


def solution(mesh):
    return jax.shard_map(
        body,
        mesh=mesh,
        in_specs=(
            P(None, "space"),
            P("tm", None, "space"),
            P("tm", None, "space"),
            P(),
            P(),
            P("space"),
            P("space"),
            P(None, "space"),
            P(None, "space"),
        ),
        out_specs=P("tm", None, "space"),
        check_vma=False,
    )
```

```python
import functools
import jax
import jax.numpy as jnp
from jax import lax
from jax.experimental import pallas as pl
from jax.experimental.pallas import tpu as pltpu
from jax.sharding import PartitionSpec as P

GX = 8
LAYER = 64
DOF = 64
COARSEN = 4
HALO = 4
MESH = pl.DeviceIdType.MESH
F32 = jnp.float32
BF16 = jnp.bfloat16


def halves(x):
    hi = x.astype(BF16)
    return hi, (x - hi.astype(F32)).astype(BF16)


def thirds(x):
    hi = x.astype(BF16)
    rest = x - hi.astype(F32)
    mid = rest.astype(BF16)
    return hi, mid, (rest - mid.astype(F32)).astype(BF16)


def times_t(a, b):
    return lax.dot_general(a, b, (((1,), (1,)), ((), ())), preferred_element_type=F32)


def select_rows(perm, values):
    hi, mid, lo = thirds(values)
    return (times_t(perm, hi) + times_t(perm, mid)) + times_t(perm, lo)


def left_lanes(rows):
    return lax.broadcasted_iota(jnp.int32, (rows, 2 * DOF), 1) < DOF


def swapped(x):
    return pltpu.roll(x, DOF, 1)


def doubled(packed):
    left = left_lanes(packed.shape[0])
    other = swapped(packed)
    return jnp.where(left, packed, other), jnp.where(left, other, packed)


def one_hot(ids_row, first, rows):
    cells = lax.broadcasted_iota(jnp.int32, (rows, ids_row.shape[1]), 0) + first
    return (ids_row == cells).astype(F32).astype(BF16)


def table_of(perm, faces):
    flags = jnp.concatenate(
        [jnp.broadcast_to(faces[f : f + 1], (DOF, faces.shape[1])) for f in range(6)], axis=0
    )
    scale = jnp.broadcast_to(faces[6:7], (2 * DOF, faces.shape[1]))
    return times_t(perm, flags.astype(BF16)), select_rows(perm, scale)


def kernel(
    layers,
    count,
    init_hbm,
    guess_hbm,
    forcing_hbm,
    volume_hbm,
    faces_hbm,
    scales_hbm,
    ids_hbm,
    walls_hbm,
    out_ref,
    init_ref,
    guess_ref,
    forcing_ref,
    volume_ref,
    faces_ref,
    scales_ref,
    ids_ref,
    walls_ref,
    weights,
    table,
    perm_ref,
    sources,
    guess_grid,
    ext_a,
    ext_b,
    split,
    prod,
    errors,
    tables_out,
    tables_in,
    guess_in,
    fine_out,
    fine_in,
    piece_out,
    piece_in,
    edge_out,
    edge_in,
    res_out,
    res_in,
    load_sem,
    tables_send,
    tables_recv,
    guess_send,
    guess_recv,
    fine_send,
    fine_recv,
    piece_send,
    piece_recv,
    edge_send,
    edge_recv,
    res_send,
    res_recv,
):
    times = lax.axis_size("tm")
    spaces = lax.axis_size("space")
    tme = lax.axis_index("tm")
    sme = lax.axis_index("space")
    own = layers * LAYER
    off = 2 * HALO
    end = off + layers
    around = [lax.rem(sme + spaces + step, spaces) for step in (1, -1, 2, -2)]

    pairs = (
        (ids_hbm, ids_ref),
        (walls_hbm, walls_ref),
        (scales_hbm, scales_ref),
        (guess_hbm, guess_ref),
        (faces_hbm, faces_ref),
        (volume_hbm, volume_ref),
        (init_hbm, init_ref),
        (forcing_hbm, forcing_ref),
    )
    loads = [pltpu.make_async_copy(a, b, load_sem.at[i]) for i, (a, b) in enumerate(pairs)]
    for copy in loads:
        copy.start()

    barrier = pltpu.get_barrier_semaphore()
    for device in around:
        pl.semaphore_signal(barrier, inc=1, device_id=(tme, device), device_id_type=MESH)
    for step in range(1, times):
        pl.semaphore_signal(
            barrier, inc=1, device_id=(lax.rem(tme + step, times), sme), device_id_type=MESH
        )

    def rows_of(layer, number=1):
        return pl.ds(layer * LAYER, number * LAYER)

    for copy in loads[:3]:
        copy.wait()
    local = ids_ref[...] - sme * own
    tables_out[0:6, :] = (1 - walls_ref[...]).astype(F32)
    tables_out[6:7, :] = scales_ref[...]
    tables_out[7:8, :] = local.astype(F32)
    perm = one_hot(local, 0, own)
    perm_ref[...] = perm

    def permuted_pair(first, second):
        return doubled(select_rows(perm_ref[...], jnp.concatenate([first, second], axis=0)))

    loads[3].wait()
    one, two = permuted_pair(guess_ref[0], guess_ref[1])
    guess_grid[0] = one
    guess_grid[1] = two
    ext_b[rows_of(off, layers), :] = one

    def pack(target, source, first, number):
        for layer in range(number):
            target[layer * LAYER : (layer + 1) * LAYER, :] = jnp.where(
                left_lanes(LAYER),
                source[rows_of(first + layer), :],
                source[rows_of(first + number + layer), :],
            )

    def unpack(source, target, first, number):
        for layer in range(number):
            one, two = doubled(source[layer * LAYER : (layer + 1) * LAYER, :])
            target[rows_of(first + layer), :] = one
            target[rows_of(first + number + layer), :] = two

    half = HALO // 2

    def fine_copies(point, step):
        return [
            pltpu.make_async_remote_copy(
                src_ref=fine_out.at[point, step, side],
                dst_ref=fine_in.at[point, step, side],
                send_sem=fine_send.at[point, step, side],
                recv_sem=fine_recv.at[point, step, side],
                device_id=(tme, around[side]),
                device_id_type=MESH,
            )
            for side in range(2)
        ]

    def send_fine(point, step, ext):
        pack(fine_out.at[point, step, 0], ext, end - HALO, half)
        pack(fine_out.at[point, step, 1], ext, off, half)
        for copy in fine_copies(point, step):
            copy.start()

    def receive_fine(point, step, ext):
        for side, copy in enumerate(fine_copies(point, step)):
            copy.wait_recv()
            unpack(fine_in.at[point, step, side], ext, off - HALO if side == 0 else end, half)

    pl.semaphore_wait(barrier, 4 + times - 1)

    guess_copy = pltpu.make_async_remote_copy(
        src_ref=guess_ref.at[count - 1],
        dst_ref=guess_in,
        send_sem=guess_send,
        recv_sem=guess_recv,
        device_id=(lax.rem(tme + 1, times), sme),
        device_id_type=MESH,
    )
    guess_copy.start()
    tables_copies = [
        pltpu.make_async_remote_copy(
            src_ref=tables_out,
            dst_ref=tables_in.at[slot],
            send_sem=tables_send.at[slot],
            recv_sem=tables_recv.at[slot],
            device_id=(tme, around[slot]),
            device_id_type=MESH,
        )
        for slot in range(4)
    ]
    for copy in tables_copies:
        copy.start()
    send_fine(1, 0, ext_b)

    for copy in loads[4:7]:
        copy.wait()

    @pl.when(tme == 0)
    def _():
        one, _ = permuted_pair(init_ref[...], init_ref[...])
        ext_a[rows_of(off, layers), :] = one
        send_fine(0, 0, ext_a)

    blocks = []
    for m in range(3):
        face = faces_ref[m]
        blocks.append(face.T)
        blocks.append(-face)
    blocks.append(volume_ref[...].T)
    blocks.append(jnp.zeros((DOF, DOF), F32))
    for pair in range(4):
        high, low = halves(jnp.concatenate(blocks[2 * pair : 2 * pair + 2], axis=1))
        weights[:, pair * 2 * DOF : (pair + 1) * 2 * DOF] = jnp.concatenate(
            [high, high, low, low], axis=0
        )

    def fill_table(first, number, hot, faces):
        flags, scale = table_of(hot, faces)
        table[rows_of(first, number), 0 : 6 * DOF] = flags
        table[rows_of(first, number), 6 * DOF : 8 * DOF] = scale

    fill_table(off - 1, layers, perm, tables_out[...])
    loads[7].wait()
    for step in range(COARSEN):
        one, two = permuted_pair(forcing_ref[step], forcing_ref[COARSEN + step])
        sources[0, step] = one
        sources[1, step] = two

    reach = 2 * HALO - 1 - layers
    spans = (
        (off - 1 - layers, 0, layers),
        (end - 1, 0, layers),
        (0, layers - reach, reach),
        (end - 1 + layers, 0, reach),
    )
    for slot, (place, begin, number) in enumerate(spans):
        tables_copies[slot].wait_recv()
        faces = tables_in[slot]
        hot = one_hot(faces[7:8].astype(jnp.int32), begin * LAYER, number * LAYER)
        fill_table(place, number, hot, faces)

    guess_copy.wait_recv()

    @pl.when(tme > 0)
    def _():
        one, _ = permuted_pair(guess_in[...], guess_in[...])
        ext_a[rows_of(off, layers), :] = one
        send_fine(0, 0, ext_a)

    def product(stage, zspan, xyspan):
        low, high = zspan
        rows = split[stage, low * LAYER : high * LAYER, :]
        prod[stage, low * LAYER : high * LAYER, 4 * DOF :] = jnp.dot(
            jnp.concatenate([rows, rows], axis=1),
            weights[:, 4 * DOF :],
            preferred_element_type=F32,
        )
        low, high = xyspan
        rows = split[stage, low * LAYER : high * LAYER, :]
        prod[stage, low * LAYER : high * LAYER, : 4 * DOF] = jnp.dot(
            jnp.concatenate([rows, rows], axis=1),
            weights[:, : 4 * DOF],
            preferred_element_type=F32,
        )

    def combined(stage, layer):
        base = layer * LAYER
        here = slice(base, base + LAYER)
        left = left_lanes(LAYER)
        left3 = left.reshape(LAYER // GX, GX, 2 * DOF)
        px = prod[stage, here, 0 : 2 * DOF].reshape(LAYER // GX, GX, 2 * DOF)
        xs = jnp.where(left3, pltpu.roll(px, GX - 1, 1), pltpu.roll(px, 1, 1))
        py = prod[stage, here, 2 * DOF : 4 * DOF].reshape(LAYER // GX, GX, 2 * DOF)
        ys = jnp.where(
            left3,
            jnp.concatenate([py[1:], py[:1]], axis=0),
            jnp.concatenate([py[-1:], py[:-1]], axis=0),
        )
        zs = jnp.where(
            left,
            prod[stage, base + LAYER : base + 2 * LAYER, 4 * DOF : 6 * DOF],
            prod[stage, base - LAYER : base, 4 * DOF : 6 * DOF],
        )
        own_term = prod[stage, here, 6 * DOF : 8 * DOF]
        tab = slice(base - LAYER, base)
        total = (
            table[tab, 0 : 2 * DOF] * xs.reshape(LAYER, 2 * DOF)
            + table[tab, 2 * DOF : 4 * DOF] * ys.reshape(LAYER, 2 * DOF)
        ) + (
            table[tab, 4 * DOF : 6 * DOF] * zs
            + table[tab, 6 * DOF : 8 * DOF] * own_term
        )
        return total + swapped(total)

    def store_split(stage, layer, value):
        low = value - value.astype(BF16).astype(F32)
        split[stage, layer * LAYER : (layer + 1) * LAYER, :] = jnp.where(
            left_lanes(LAYER), value, low
        ).astype(BF16)

    def advance(x, size, stage, layer, finish):
        here = slice(layer * LAYER, (layer + 1) * LAYER)
        value = x[here, :] + size / (4 - stage) * combined(stage, layer)
        if stage < 3:
            store_split(stage + 1, layer, value)
        else:
            finish(layer, value)

    def inner_step(x, size, finish):
        low, high = off - HALO, end + HALO
        for layer in range(low, high):
            store_split(0, layer, x[layer * LAYER : (layer + 1) * LAYER, :])
        for stage in range(4):
            product(stage, (low + stage, high - stage), (low + stage + 1, high - stage - 1))
            for layer in range(low + stage + 1, high - stage - 1):
                advance(x, size, stage, layer, finish)

    def outer_step(x, size, finish):
        last = end + 2 * HALO
        for layer in (*range(HALO), *range(last - HALO, last)):
            store_split(0, layer, x[layer * LAYER : (layer + 1) * LAYER, :])
        for stage in range(4):
            sides = (
                ((stage, stage + HALO), (stage + 1, stage + 1 + HALO)),
                (
                    (last - stage - HALO, last - stage),
                    (last - stage - 1 - HALO, last - stage - 1),
                ),
            )
            for zspan, xyspan in sides:
                product(stage, zspan, xyspan)
            for _, xyspan in sides:
                for layer in range(*xyspan):
                    advance(x, size, stage, layer, finish)

    def residual_copies(index):
        point = count * tme + index
        result = []
        for step in range(times - 1, 0, -1):
            result.append((
                step,
                pltpu.make_async_remote_copy(
                    src_ref=res_out.at[index],
                    dst_ref=res_in.at[point],
                    send_sem=res_send.at[index, step],
                    recv_sem=res_recv.at[point],
                    device_id=(lax.rem(tme + step, times), sme),
                    device_id_type=MESH,
                ),
            ))
        return result

    def fine(step, carry):
        for point, ext in ((1, ext_b), (0, ext_a)):
            receive_fine(point, step, ext)

            def finish(layer, value):
                inside = rows_of(layer - off)
                ext[rows_of(layer), :] = value + sources[point, step, inside, :]

            inner_step(ext, 1.0, finish)

            @pl.when(step < COARSEN - 1)
            def _():
                send_fine(point, step + 1, ext)

            @pl.when(step == COARSEN - 1)
            def _():
                index = count * tme + point
                errors[index] = ext[rows_of(off, layers), :] - guess_grid[point]
                pack(res_out.at[point], errors.at[index], 0, layers // 2)
                for distance, copy in residual_copies(point):

                    @pl.when(tme + distance < times)
                    def _():
                        copy.start()

        return carry

    lax.fori_loop(0, COARSEN, fine, 0)

    final = count * tme + count - 1

    def take_residual(point):
        @pl.when(point < count * tme)
        def _():
            pltpu.make_async_remote_copy(
                src_ref=res_out.at[0],
                dst_ref=res_in.at[point],
                send_sem=res_send.at[0, 0],
                recv_sem=res_recv.at[point],
                device_id=(lax.rem(tme + 1, times), sme),
                device_id_type=MESH,
            ).wait_recv()
            unpack(res_in.at[point], errors.at[point], 0, layers // 2)

    def edge_copies(point):
        return [
            pltpu.make_async_remote_copy(
                src_ref=edge_out.at[point, side],
                dst_ref=edge_in.at[point, side],
                send_sem=edge_send.at[point, side],
                recv_sem=edge_recv.at[point, side],
                device_id=(tme, around[side]),
                device_id_type=MESH,
            )
            for side in range(2)
        ]

    def send_edges(point):
        pack(edge_out.at[point, 0], errors.at[point], layers - HALO, half)
        pack(edge_out.at[point, 1], errors.at[point], 0, half)
        for copy in edge_copies(point):
            copy.start()

    def piece_copies(point):
        return [
            pltpu.make_async_remote_copy(
                src_ref=piece_out.at[point, (0, 1, 1, 0)[slot]],
                dst_ref=piece_in.at[point, slot],
                send_sem=piece_send.at[point, slot],
                recv_sem=piece_recv.at[point, slot],
                device_id=(tme, around[slot]),
                device_id_type=MESH,
            )
            for slot in range(4)
        ]

    def send_pieces(point):
        pack(piece_out.at[point, 0], ext_a, off, 1)
        pack(piece_out.at[point, 1], ext_a, end - 2, 1)
        for copy in piece_copies(point):
            copy.start()

    def receive_pieces(point):
        places = (off - layers, end + layers - 2, 0, end + layers)
        for slot, copy in enumerate(piece_copies(point)):
            copy.wait_recv()
            unpack(piece_in.at[point, slot], ext_a, places[slot], 1)

    def receive_edges(point, place):
        for side, copy in enumerate(edge_copies(point)):
            copy.wait_recv()
            place(side, edge_in.at[point, side])

    take_residual(0)
    send_edges(0)
    ext_a[rows_of(off, layers), :] = errors[0]

    @pl.when(final > 1)
    def _():
        send_pieces(0)

    receive_edges(0, lambda side, ref: unpack(ref, ext_a, off - HALO if side == 0 else end, half))

    def coarse(point, carry):
        take_residual(point)

        @pl.when(point < final)
        def _():
            send_edges(point)

        def finish(layer, value):
            inside = rows_of(layer - off)
            value = value + errors[point, inside, :]
            ext_a[rows_of(layer), :] = value
            errors[point, inside, :] = value

        inner_step(ext_a, float(COARSEN), finish)

        @pl.when(point < final - 1)
        def _():
            send_pieces(point)

        @pl.when(point < final)
        def _():
            receive_pieces(point - 1)
            receive_edges(
                point, lambda side, ref: unpack(ref, ext_b, off - HALO if side == 0 else end, half)
            )

            def finish_outer(layer, value):
                ext_a[rows_of(layer), :] = value + ext_b[rows_of(layer), :]

            outer_step(ext_a, float(COARSEN), finish_outer)

        return carry

    lax.fori_loop(1, final + 1, coarse, 0)

    packed = jnp.where(left_lanes(own), errors[final - 1], errors[final])
    parts = [
        lax.dot_general(part, perm_ref[...], (((0,), (0,)), ((), ())), preferred_element_type=F32)
        for part in thirds(packed)
    ]
    result = (parts[0] + parts[1]) + parts[2]
    out_ref[0] = result[:DOF]
    out_ref[1] = result[DOF:]

    guess_copy.wait_send()
    for copy in tables_copies:
        copy.wait_send()

    def fine_done(step, carry):
        for point in range(2):
            for copy in fine_copies(point, step):
                copy.wait_send()
        return carry

    lax.fori_loop(0, COARSEN, fine_done, 0)
    for index in range(2):
        for distance, copy in residual_copies(index):

            @pl.when(tme + distance < times)
            def _():
                copy.wait_send()

    def sweep_done(point, carry):
        for copy in edge_copies(point):
            copy.wait_send()

        @pl.when(point < final - 1)
        def _():
            for copy in piece_copies(point):
                copy.wait_send()

        return carry

    lax.fori_loop(0, final, sweep_done, 0)


def body(init_state, guess, forcing, volume_block, face_blocks, elem_scales, element_ids, neighbours, walls):
    own = element_ids.shape[0]
    layers = own // LAYER
    count = guess.shape[0]
    times = lax.axis_size("tm")
    points = times * count
    ext = (layers + 4 * HALO) * LAYER
    wide = 2 * DOF
    vmem = pltpu.VMEM
    dma = pltpu.SemaphoreType.DMA
    errors = pl.pallas_call(
        functools.partial(kernel, layers, count),
        out_shape=jax.ShapeDtypeStruct(guess.shape, F32),
        in_specs=[pl.BlockSpec(memory_space=pl.ANY)] * 8,
        out_specs=pl.BlockSpec(memory_space=pltpu.VMEM),
        scratch_shapes=[
            vmem(init_state.shape, F32),
            vmem(guess.shape, F32),
            vmem(forcing.shape, F32),
            vmem(volume_block.shape, F32),
            vmem(face_blocks.shape, F32),
            vmem((1, own), F32),
            vmem((1, own), jnp.int32),
            vmem(walls.shape, jnp.int32),
            vmem((4 * DOF, 8 * DOF), BF16),
            vmem((ext - 2 * LAYER, 8 * DOF), F32),
            vmem((own, own), BF16),
            vmem((2, COARSEN, own, wide), F32),
            vmem((2, own, wide), F32),
            vmem((ext, wide), F32),
            vmem((ext, wide), F32),
            vmem((4, ext, wide), BF16),
            vmem((4, ext, 8 * DOF), F32),
            vmem((points, own, wide), F32),
            vmem((8, own), F32),
            vmem((4, 8, own), F32),
            vmem((DOF, own), F32),
            vmem((2, COARSEN, 2, HALO // 2 * LAYER, wide), F32),
            vmem((2, COARSEN, 2, HALO // 2 * LAYER, wide), F32),
            vmem((points, 2, LAYER, wide), F32),
            vmem((points, 4, LAYER, wide), F32),
            vmem((points, 2, HALO // 2 * LAYER, wide), F32),
            vmem((points, 2, HALO // 2 * LAYER, wide), F32),
            vmem((2, own // 2, wide), F32),
            vmem((points, own // 2, wide), F32),
            dma((8,)),
            dma((4,)),
            dma((4,)),
            dma,
            dma,
            dma((2, COARSEN, 2)),
            dma((2, COARSEN, 2)),
            dma((points, 4)),
            dma((points, 4)),
            dma((points, 2)),
            dma((points, 2)),
            dma((2, times)),
            dma((points,)),
        ],
        compiler_params=pltpu.CompilerParams(
            collective_id=0, has_side_effects=True, vmem_limit_bytes=56 * 1024 * 1024
        ),
    )(
        init_state,
        guess,
        forcing,
        volume_block,
        face_blocks,
        elem_scales.reshape(1, own),
        element_ids.reshape(1, own),
        walls,
    )
    return guess + errors


def solution(mesh):
    return jax.shard_map(
        body,
        mesh=mesh,
        in_specs=(
            P(None, "space"),
            P("tm", None, "space"),
            P("tm", None, "space"),
            P(),
            P(),
            P("space"),
            P("space"),
            P(None, "space"),
            P(None, "space"),
        ),
        out_specs=P("tm", None, "space"),
        check_vma=False,
    )
```

```python
import functools
import jax
import jax.numpy as jnp
from jax import lax
from jax.experimental import pallas as pl
from jax.experimental.pallas import tpu as pltpu
from jax.sharding import PartitionSpec as P

GX = 8
LAYER = 64
DOF = 64
COARSEN = 4
HALO = 4
MESH = pl.DeviceIdType.MESH
F32 = jnp.float32
BF16 = jnp.bfloat16


def halves(x):
    hi = x.astype(BF16)
    return hi, (x - hi.astype(F32)).astype(BF16)


def thirds(x):
    hi = x.astype(BF16)
    rest = x - hi.astype(F32)
    mid = rest.astype(BF16)
    return hi, mid, (rest - mid.astype(F32)).astype(BF16)


def times_t(a, b):
    return lax.dot_general(a, b, (((1,), (1,)), ((), ())), preferred_element_type=F32)


def select_rows(perm, values):
    hi, mid, lo = thirds(values)
    return (times_t(perm, hi) + times_t(perm, mid)) + times_t(perm, lo)


def left_lanes(rows):
    return lax.broadcasted_iota(jnp.int32, (rows, 2 * DOF), 1) < DOF


def swapped(x):
    return pltpu.roll(x, DOF, 1)


def doubled(packed):
    left = left_lanes(packed.shape[0])
    other = swapped(packed)
    return jnp.where(left, packed, other), jnp.where(left, other, packed)


def one_hot(ids_row, first, rows):
    cells = lax.broadcasted_iota(jnp.int32, (rows, ids_row.shape[1]), 0) + first
    return (ids_row == cells).astype(F32).astype(BF16)


def table_of(perm, faces):
    flags = jnp.concatenate(
        [jnp.broadcast_to(faces[f : f + 1], (DOF, faces.shape[1])) for f in range(6)], axis=0
    )
    scale = jnp.broadcast_to(faces[6:7], (2 * DOF, faces.shape[1]))
    return times_t(perm, flags.astype(BF16)), select_rows(perm, scale)


def kernel(
    layers,
    count,
    init_hbm,
    guess_hbm,
    forcing_hbm,
    volume_hbm,
    faces_hbm,
    scales_hbm,
    ids_hbm,
    walls_hbm,
    out_ref,
    init_ref,
    guess_ref,
    forcing_ref,
    volume_ref,
    faces_ref,
    scales_ref,
    ids_ref,
    walls_ref,
    weights,
    table,
    perm_ref,
    sources,
    guess_grid,
    exts,
    spare,
    split,
    prod,
    errors,
    tables_out,
    tables_in,
    guess_in,
    block_out,
    block_in,
    strip_out,
    strip_in,
    force_out,
    force_in,
    piece_out,
    piece_in,
    edge_out,
    edge_in,
    res_out,
    res_in,
    load_sem,
    tables_send,
    tables_recv,
    guess_send,
    guess_recv,
    block_send,
    block_recv,
    strip_send,
    strip_recv,
    force_send,
    force_recv,
    piece_send,
    piece_recv,
    edge_send,
    edge_recv,
    res_send,
    res_recv,
):
    times = lax.axis_size("tm")
    spaces = lax.axis_size("space")
    tme = lax.axis_index("tm")
    sme = lax.axis_index("space")
    own = layers * LAYER
    ext_a = exts.at[0]
    off = 2 * HALO
    end = off + layers
    around = [lax.rem(sme + spaces + step, spaces) for step in (1, -1, 2, -2)]

    pairs = (
        (ids_hbm, ids_ref),
        (walls_hbm, walls_ref),
        (scales_hbm, scales_ref),
        (guess_hbm, guess_ref),
        (faces_hbm, faces_ref),
        (volume_hbm, volume_ref),
        (init_hbm, init_ref),
        (forcing_hbm, forcing_ref),
    )
    loads = [pltpu.make_async_copy(a, b, load_sem.at[i]) for i, (a, b) in enumerate(pairs)]
    for copy in loads:
        copy.start()

    barrier = pltpu.get_barrier_semaphore()
    for device in around:
        pl.semaphore_signal(barrier, inc=1, device_id=(tme, device), device_id_type=MESH)
    for step in range(1, times):
        pl.semaphore_signal(
            barrier, inc=1, device_id=(lax.rem(tme + step, times), sme), device_id_type=MESH
        )

    def rows_of(layer, number=1):
        return pl.ds(layer * LAYER, number * LAYER)

    for copy in loads[:3]:
        copy.wait()
    local = ids_ref[...].reshape(1, own) - sme * own
    tables_out[0:6, :] = (1 - walls_ref[...]).astype(F32)
    tables_out[6:7, :] = scales_ref[...].reshape(1, own)
    tables_out[7:8, :] = local.astype(F32)
    perm = one_hot(local, 0, own)
    perm_ref[...] = perm

    def permuted_pair(first, second):
        return doubled(select_rows(perm_ref[...], jnp.concatenate([first, second], axis=0)))

    loads[3].wait()
    one, two = permuted_pair(guess_ref[0], guess_ref[1])
    guess_grid[0] = one
    guess_grid[1] = two
    exts[1, rows_of(off, layers), :] = one

    def pack(target, source, first, number):
        for layer in range(number):
            target[layer * LAYER : (layer + 1) * LAYER, :] = jnp.where(
                left_lanes(LAYER),
                source[rows_of(first + layer), :],
                source[rows_of(first + number + layer), :],
            )

    def unpack(source, target, first, number):
        for layer in range(number):
            one, two = doubled(source[layer * LAYER : (layer + 1) * LAYER, :])
            target[rows_of(first + layer), :] = one
            target[rows_of(first + number + layer), :] = two

    half = HALO // 2

    def remote(source, target, send, recv, slot):
        return pltpu.make_async_remote_copy(
            src_ref=source,
            dst_ref=target,
            send_sem=send,
            recv_sem=recv,
            device_id=(tme, around[slot]),
            device_id_type=MESH,
        )

    def state_copies(point, turn):
        copies = [
            remote(
                block_out.at[point, turn],
                block_in.at[point, turn, side],
                block_send.at[point, turn, side],
                block_recv.at[point, turn, side],
                side,
            )
            for side in range(2)
        ]
        return copies + [
            remote(
                strip_out.at[point, turn, side],
                strip_in.at[point, turn, side],
                strip_send.at[point, turn, side],
                strip_recv.at[point, turn, side],
                2 + side,
            )
            for side in range(2)
        ]

    def send_state(point, turn):
        ext = exts.at[point]
        pack(block_out.at[point, turn], ext, off, layers // 2)
        pack(strip_out.at[point, turn, 0], ext, end - 2, 1)
        pack(strip_out.at[point, turn, 1], ext, off, 1)
        for copy in state_copies(point, turn):
            copy.start()

    def receive_state(point, turn):
        ext = exts.at[point]
        copies = state_copies(point, turn)
        for copy in copies:
            copy.wait_recv()
        unpack(block_in.at[point, turn, 0], ext, off - layers, layers // 2)
        unpack(block_in.at[point, turn, 1], ext, end, layers // 2)
        unpack(strip_in.at[point, turn, 0], ext, off - layers - 2, 1)
        unpack(strip_in.at[point, turn, 1], ext, end + layers, 1)

    def force_copies(point, turn):
        return [
            remote(
                force_out.at[point, turn, side],
                force_in.at[point, turn, side],
                force_send.at[point, turn, side],
                force_recv.at[point, turn, side],
                side,
            )
            for side in range(2)
        ]

    def send_force(point, turn):
        source = sources.at[point, 2 * turn]
        pack(force_out.at[point, turn, 0], source, layers, half)
        pack(force_out.at[point, turn, 1], source, HALO, half)
        for copy in force_copies(point, turn):
            copy.start()

    def receive_force(point, turn):
        for side, copy in enumerate(force_copies(point, turn)):
            copy.wait_recv()
            unpack(
                force_in.at[point, turn, side],
                sources.at[point, 2 * turn],
                0 if side == 0 else HALO + layers,
                half,
            )

    for copy in loads[4:7]:
        copy.wait()

    @pl.when(tme == 0)
    def _():
        one, _ = permuted_pair(init_ref[...], init_ref[...])
        exts[0, rows_of(off, layers), :] = one

    pl.semaphore_wait(barrier, 4 + times - 1)

    guess_copy = pltpu.make_async_remote_copy(
        src_ref=guess_ref.at[count - 1],
        dst_ref=guess_in,
        send_sem=guess_send,
        recv_sem=guess_recv,
        device_id=(lax.rem(tme + 1, times), sme),
        device_id_type=MESH,
    )
    guess_copy.start()
    tables_copies = [
        pltpu.make_async_remote_copy(
            src_ref=tables_out,
            dst_ref=tables_in.at[slot],
            send_sem=tables_send.at[slot],
            recv_sem=tables_recv.at[slot],
            device_id=(tme, around[slot]),
            device_id_type=MESH,
        )
        for slot in range(4)
    ]
    for copy in tables_copies:
        copy.start()

    @pl.when(tme == 0)
    def _():
        send_state(0, 0)

    send_state(1, 0)
    loads[7].wait()
    for step in (0, 2, 1, 3):
        one, two = permuted_pair(forcing_ref[step], forcing_ref[COARSEN + step])
        sources[0, step, rows_of(HALO, layers), :] = one
        sources[1, step, rows_of(HALO, layers), :] = two
        if step == 0:
            send_force(1, 0)
            send_force(0, 0)

    blocks = []
    for m in range(3):
        face = faces_ref[m]
        blocks.append(face.T)
        blocks.append(-face)
    blocks.append(volume_ref[...].T)
    blocks.append(jnp.zeros((DOF, DOF), F32))
    for pair in range(4):
        high, low = halves(jnp.concatenate(blocks[2 * pair : 2 * pair + 2], axis=1))
        weights[:, pair * 2 * DOF : (pair + 1) * 2 * DOF] = jnp.concatenate(
            [high, high, low, low], axis=0
        )

    def fill_table(first, number, hot, faces):
        flags, scale = table_of(hot, faces)
        table[rows_of(first, number), 0 : 6 * DOF] = flags
        table[rows_of(first, number), 6 * DOF : 8 * DOF] = scale

    fill_table(off - 1, layers, perm, tables_out[...])
    reach = 2 * HALO - 1 - layers
    spans = (
        (off - 1 - layers, 0, layers),
        (end - 1, 0, layers),
        (0, layers - reach, reach),
        (end - 1 + layers, 0, reach),
    )
    for slot, (place, begin, number) in enumerate(spans):
        tables_copies[slot].wait_recv()
        faces = tables_in[slot]
        hot = one_hot(faces[7:8].astype(jnp.int32), begin * LAYER, number * LAYER)
        fill_table(place, number, hot, faces)

    guess_copy.wait_recv()

    @pl.when(tme > 0)
    def _():
        one, _ = permuted_pair(guess_in[...], guess_in[...])
        exts[0, rows_of(off, layers), :] = one
        send_state(0, 0)

    send_force(1, 1)
    send_force(0, 1)

    def product(stage, zspan, xyspan):
        low, high = zspan
        rows = split[stage, low * LAYER : high * LAYER, :]
        prod[stage, low * LAYER : high * LAYER, 4 * DOF :] = jnp.dot(
            jnp.concatenate([rows, rows], axis=1),
            weights[:, 4 * DOF :],
            preferred_element_type=F32,
        )
        low, high = xyspan
        rows = split[stage, low * LAYER : high * LAYER, :]
        prod[stage, low * LAYER : high * LAYER, : 4 * DOF] = jnp.dot(
            jnp.concatenate([rows, rows], axis=1),
            weights[:, : 4 * DOF],
            preferred_element_type=F32,
        )

    def combined(stage, layer):
        base = layer * LAYER
        here = slice(base, base + LAYER)
        left = left_lanes(LAYER)
        left3 = left.reshape(LAYER // GX, GX, 2 * DOF)
        px = prod[stage, here, 0 : 2 * DOF].reshape(LAYER // GX, GX, 2 * DOF)
        xs = jnp.where(left3, pltpu.roll(px, GX - 1, 1), pltpu.roll(px, 1, 1))
        py = prod[stage, here, 2 * DOF : 4 * DOF].reshape(LAYER // GX, GX, 2 * DOF)
        ys = jnp.where(
            left3,
            jnp.concatenate([py[1:], py[:1]], axis=0),
            jnp.concatenate([py[-1:], py[:-1]], axis=0),
        )
        zs = jnp.where(
            left,
            prod[stage, base + LAYER : base + 2 * LAYER, 4 * DOF : 6 * DOF],
            prod[stage, base - LAYER : base, 4 * DOF : 6 * DOF],
        )
        own_term = prod[stage, here, 6 * DOF : 8 * DOF]
        tab = slice(base - LAYER, base)
        total = (
            table[tab, 0 : 2 * DOF] * xs.reshape(LAYER, 2 * DOF)
            + table[tab, 2 * DOF : 4 * DOF] * ys.reshape(LAYER, 2 * DOF)
        ) + (
            table[tab, 4 * DOF : 6 * DOF] * zs
            + table[tab, 6 * DOF : 8 * DOF] * own_term
        )
        return total + swapped(total)

    def store_split(stage, layer, value):
        low = value - value.astype(BF16).astype(F32)
        split[stage, layer * LAYER : (layer + 1) * LAYER, :] = jnp.where(
            left_lanes(LAYER), value, low
        ).astype(BF16)

    def advance(x, size, stage, layer, finish):
        here = slice(layer * LAYER, (layer + 1) * LAYER)
        value = x[here, :] + size / (4 - stage) * combined(stage, layer)
        if stage < 3:
            store_split(stage + 1, layer, value)
        else:
            finish(layer, value)

    def whole_step(x, size, low, high, finish):
        for layer in range(low, high):
            store_split(0, layer, x[layer * LAYER : (layer + 1) * LAYER, :])
        for stage in range(4):
            product(stage, (low + stage, high - stage), (low + stage + 1, high - stage - 1))
            for layer in range(low + stage + 1, high - stage - 1):
                advance(x, size, stage, layer, finish)

    def inner_step(x, size, finish):
        whole_step(x, size, off - HALO, end + HALO, finish)

    def outer_step(x, size, finish):
        last = end + 2 * HALO
        for layer in (*range(HALO), *range(last - HALO, last)):
            store_split(0, layer, x[layer * LAYER : (layer + 1) * LAYER, :])
        for stage in range(4):
            sides = (
                ((stage, stage + HALO), (stage + 1, stage + 1 + HALO)),
                (
                    (last - stage - HALO, last - stage),
                    (last - stage - 1 - HALO, last - stage - 1),
                ),
            )
            for zspan, xyspan in sides:
                product(stage, zspan, xyspan)
            for _, xyspan in sides:
                for layer in range(*xyspan):
                    advance(x, size, stage, layer, finish)

    def residual_copies(index):
        point = count * tme + index
        result = []
        for step in range(times - 1, 0, -1):
            result.append((
                step,
                pltpu.make_async_remote_copy(
                    src_ref=res_out.at[index],
                    dst_ref=res_in.at[point],
                    send_sem=res_send.at[index, step],
                    recv_sem=res_recv.at[point],
                    device_id=(lax.rem(tme + step, times), sme),
                    device_id_type=MESH,
                ),
            ))
        return result

    def fine(index, carry):
        turn = index // 2
        point = lax.rem(index + jnp.minimum(tme, 1), 2)
        ext = exts.at[point]
        receive_state(point, turn)
        receive_force(point, turn)

        def finish(step):
            def store(layer, value):
                there = rows_of(layer - off + HALO)
                ext[rows_of(layer), :] = value + sources[point, 2 * turn + step, there, :]

            return store

        whole_step(ext, 1.0, off - 2 * HALO, end + 2 * HALO, finish(0))
        inner_step(ext, 1.0, finish(1))

        @pl.when(turn == 0)
        def _():
            send_state(point, 1)

        @pl.when(turn == 1)
        def _():
            place = count * tme + point
            errors[place] = ext[rows_of(off, layers), :] - guess_grid[point]
            pack(res_out.at[point], errors.at[place], 0, layers // 2)
            for distance, copy in residual_copies(point):

                @pl.when(tme + distance < times)
                def _():
                    copy.start()

        return carry

    lax.fori_loop(0, 4, fine, 0)

    final = count * tme + count - 1

    def take_residual(point):
        @pl.when(point < count * tme)
        def _():
            pltpu.make_async_remote_copy(
                src_ref=res_out.at[0],
                dst_ref=res_in.at[point],
                send_sem=res_send.at[0, 0],
                recv_sem=res_recv.at[point],
                device_id=(lax.rem(tme + 1, times), sme),
                device_id_type=MESH,
            ).wait_recv()
            unpack(res_in.at[point], errors.at[point], 0, layers // 2)

    def edge_copies(point):
        return [
            pltpu.make_async_remote_copy(
                src_ref=edge_out.at[point, side],
                dst_ref=edge_in.at[point, side],
                send_sem=edge_send.at[point, side],
                recv_sem=edge_recv.at[point, side],
                device_id=(tme, around[side]),
                device_id_type=MESH,
            )
            for side in range(2)
        ]

    def send_edges(point):
        pack(edge_out.at[point, 0], errors.at[point], layers - HALO, half)
        pack(edge_out.at[point, 1], errors.at[point], 0, half)
        for copy in edge_copies(point):
            copy.start()

    def piece_copies(point):
        return [
            pltpu.make_async_remote_copy(
                src_ref=piece_out.at[point, (0, 1, 1, 0)[slot]],
                dst_ref=piece_in.at[point, slot],
                send_sem=piece_send.at[point, slot],
                recv_sem=piece_recv.at[point, slot],
                device_id=(tme, around[slot]),
                device_id_type=MESH,
            )
            for slot in range(4)
        ]

    def send_pieces(point):
        pack(piece_out.at[point, 0], ext_a, off, 1)
        pack(piece_out.at[point, 1], ext_a, end - 2, 1)
        for copy in piece_copies(point):
            copy.start()

    def receive_pieces(point):
        places = (off - layers, end + layers - 2, 0, end + layers)
        for slot, copy in enumerate(piece_copies(point)):
            copy.wait_recv()
            unpack(piece_in.at[point, slot], ext_a, places[slot], 1)

    def receive_edges(point, place):
        for side, copy in enumerate(edge_copies(point)):
            copy.wait_recv()
            place(side, edge_in.at[point, side])

    def pass_residual(point):
        @pl.when(point <= final)
        def _():
            take_residual(point)

        @pl.when(point < final)
        def _():
            send_edges(point)

    pass_residual(0)
    ext_a[rows_of(off, layers), :] = errors[0]

    @pl.when(final > 1)
    def _():
        send_pieces(0)

    pass_residual(1)
    pass_residual(2)

    receive_edges(0, lambda side, ref: unpack(ref, ext_a, off - HALO if side == 0 else end, half))

    def coarse(point, carry):
        def finish(layer, value):
            inside = rows_of(layer - off)
            value = value + errors[point, inside, :]
            ext_a[rows_of(layer), :] = value
            errors[point, inside, :] = value

        inner_step(ext_a, float(COARSEN), finish)

        @pl.when(point < final - 1)
        def _():
            send_pieces(point)

        pass_residual(point + 2)

        @pl.when(point < final)
        def _():
            receive_pieces(point - 1)
            receive_edges(
                point, lambda side, ref: unpack(ref, spare, off - HALO if side == 0 else end, half)
            )

            def finish_outer(layer, value):
                ext_a[rows_of(layer), :] = value + spare[rows_of(layer), :]

            outer_step(ext_a, float(COARSEN), finish_outer)

        return carry

    lax.fori_loop(1, final + 1, coarse, 0)

    packed = jnp.where(left_lanes(own), errors[final - 1], errors[final])
    parts = [
        lax.dot_general(part, perm_ref[...], (((0,), (0,)), ((), ())), preferred_element_type=F32)
        for part in thirds(packed)
    ]
    result = (parts[0] + parts[1]) + parts[2]
    out_ref[0] = result[:DOF]
    out_ref[1] = result[DOF:]

    guess_copy.wait_send()
    for copy in tables_copies:
        copy.wait_send()

    for point in range(2):
        for turn in range(2):
            for copy in state_copies(point, turn) + force_copies(point, turn):
                copy.wait_send()
    for index in range(2):
        for distance, copy in residual_copies(index):

            @pl.when(tme + distance < times)
            def _():
                copy.wait_send()

    def sweep_done(point, carry):
        for copy in edge_copies(point):
            copy.wait_send()

        @pl.when(point < final - 1)
        def _():
            for copy in piece_copies(point):
                copy.wait_send()

        return carry

    lax.fori_loop(0, final, sweep_done, 0)


def body(init_state, guess, forcing, volume_block, face_blocks, elem_scales, element_ids, neighbours, walls):
    own = element_ids.shape[0]
    layers = own // LAYER
    count = guess.shape[0]
    times = lax.axis_size("tm")
    points = times * count
    ext = (layers + 4 * HALO) * LAYER
    wide = 2 * DOF
    vmem = pltpu.VMEM
    dma = pltpu.SemaphoreType.DMA
    errors = pl.pallas_call(
        functools.partial(kernel, layers, count),
        out_shape=jax.ShapeDtypeStruct(guess.shape, F32),
        in_specs=[pl.BlockSpec(memory_space=pl.ANY)] * 8,
        out_specs=pl.BlockSpec(memory_space=pltpu.VMEM),
        scratch_shapes=[
            vmem(init_state.shape, F32),
            vmem(guess.shape, F32),
            vmem(forcing.shape, F32),
            vmem(volume_block.shape, F32),
            vmem(face_blocks.shape, F32),
            vmem((own,), F32),
            vmem((own,), jnp.int32),
            vmem(walls.shape, jnp.int32),
            vmem((4 * DOF, 8 * DOF), BF16),
            vmem((ext - 2 * LAYER, 8 * DOF), F32),
            vmem((own, own), BF16),
            vmem((2, COARSEN, own + 2 * HALO * LAYER, wide), F32),
            vmem((2, own, wide), F32),
            vmem((2, ext, wide), F32),
            vmem((ext, wide), F32),
            vmem((4, ext, wide), BF16),
            vmem((4, ext, 8 * DOF), F32),
            vmem((points, own, wide), F32),
            vmem((8, own), F32),
            vmem((4, 8, own), F32),
            vmem((DOF, own), F32),
            vmem((2, 2, own // 2, wide), F32),
            vmem((2, 2, 2, own // 2, wide), F32),
            vmem((2, 2, 2, LAYER, wide), F32),
            vmem((2, 2, 2, LAYER, wide), F32),
            vmem((2, 2, 2, HALO // 2 * LAYER, wide), F32),
            vmem((2, 2, 2, HALO // 2 * LAYER, wide), F32),
            vmem((points, 2, LAYER, wide), F32),
            vmem((points, 4, LAYER, wide), F32),
            vmem((points, 2, HALO // 2 * LAYER, wide), F32),
            vmem((points, 2, HALO // 2 * LAYER, wide), F32),
            vmem((2, own // 2, wide), F32),
            vmem((points, own // 2, wide), F32),
            dma((8,)),
            dma((4,)),
            dma((4,)),
            dma,
            dma,
            dma((2, 2, 2)),
            dma((2, 2, 2)),
            dma((2, 2, 2)),
            dma((2, 2, 2)),
            dma((2, 2, 2)),
            dma((2, 2, 2)),
            dma((points, 4)),
            dma((points, 4)),
            dma((points, 2)),
            dma((points, 2)),
            dma((2, times)),
            dma((points,)),
        ],
        compiler_params=pltpu.CompilerParams(
            collective_id=0, has_side_effects=True, vmem_limit_bytes=56 * 1024 * 1024
        ),
    )(
        init_state,
        guess,
        forcing,
        volume_block,
        face_blocks,
        elem_scales,
        element_ids,
        walls,
    )
    return guess + errors


def solution(mesh):
    return jax.shard_map(
        body,
        mesh=mesh,
        in_specs=(
            P(None, "space"),
            P("tm", None, "space"),
            P("tm", None, "space"),
            P(),
            P(),
            P("space"),
            P("space"),
            P(None, "space"),
            P(None, "space"),
        ),
        out_specs=P("tm", None, "space"),
        check_vma=False,
    )
```

```python
import functools
import jax
import jax.numpy as jnp
from jax import lax
from jax.experimental import pallas as pl
from jax.experimental.pallas import tpu as pltpu
from jax.sharding import PartitionSpec as P

GX = 8
LAYER = 64
DOF = 64
COARSEN = 4
HALO = 4
MESH = pl.DeviceIdType.MESH
F32 = jnp.float32
BF16 = jnp.bfloat16


def halves(x):
    hi = x.astype(BF16)
    return hi, (x - hi.astype(F32)).astype(BF16)


def thirds(x):
    hi = x.astype(BF16)
    rest = x - hi.astype(F32)
    mid = rest.astype(BF16)
    return hi, mid, (rest - mid.astype(F32)).astype(BF16)


def times_t(a, b):
    return lax.dot_general(a, b, (((1,), (1,)), ((), ())), preferred_element_type=F32)


def select_rows(perm, values):
    hi, mid, lo = thirds(values)
    return (times_t(perm, hi) + times_t(perm, mid)) + times_t(perm, lo)


def left_lanes(rows):
    return lax.broadcasted_iota(jnp.int32, (rows, 2 * DOF), 1) < DOF


def swapped(x):
    return pltpu.roll(x, DOF, 1)


def doubled(packed):
    left = left_lanes(packed.shape[0])
    other = swapped(packed)
    return jnp.where(left, packed, other), jnp.where(left, other, packed)


def one_hot(ids_row, first, rows):
    cells = lax.broadcasted_iota(jnp.int32, (rows, ids_row.shape[1]), 0) + first
    return (ids_row == cells).astype(F32).astype(BF16)


def table_of(perm, faces):
    flags = jnp.concatenate(
        [jnp.broadcast_to(faces[f : f + 1], (DOF, faces.shape[1])) for f in range(6)], axis=0
    )
    scale = jnp.broadcast_to(faces[6:7], (2 * DOF, faces.shape[1]))
    return times_t(perm, flags.astype(BF16)), select_rows(perm, scale)


def kernel(
    layers,
    count,
    init_hbm,
    guess_hbm,
    forcing_hbm,
    volume_hbm,
    faces_hbm,
    scales_hbm,
    ids_hbm,
    walls_hbm,
    out_ref,
    init_ref,
    guess_ref,
    forcing_ref,
    volume_ref,
    faces_ref,
    scales_ref,
    ids_ref,
    walls_ref,
    weights,
    table,
    perm_ref,
    sources,
    guess_grid,
    exts,
    spare,
    split,
    prod,
    errors,
    tables_out,
    tables_in,
    guess_in,
    block_out,
    block_in,
    strip_out,
    strip_in,
    force_out,
    force_in,
    piece_out,
    piece_in,
    edge_out,
    edge_in,
    res_out,
    res_in,
    load_sem,
    tables_send,
    tables_recv,
    guess_send,
    guess_recv,
    block_send,
    block_recv,
    strip_send,
    strip_recv,
    force_send,
    force_recv,
    piece_send,
    piece_recv,
    edge_send,
    edge_recv,
    res_send,
    res_recv,
):
    times = lax.axis_size("tm")
    spaces = lax.axis_size("space")
    tme = lax.axis_index("tm")
    sme = lax.axis_index("space")
    own = layers * LAYER
    ext_a = exts.at[0]
    off = 2 * HALO
    end = off + layers
    around = [lax.rem(sme + spaces + step, spaces) for step in (1, -1, 2, -2)]
    heard = [sme >= 1, sme <= spaces - 2, sme >= 2, sme <= spaces - 3]
    sent = [heard[1], heard[0], heard[3], heard[2]]

    def start(copies):
        for slot, copy in copies:
            pl.when(sent[slot])(copy.start)

    def arrive(copies):
        for slot, copy in copies:
            pl.when(heard[slot])(copy.wait_recv)

    def finish_sends(copies):
        for slot, copy in copies:
            pl.when(sent[slot])(copy.wait_send)

    for slot in range(4):

        @pl.when(jnp.logical_not(heard[slot]))
        def _():
            tables_in[slot] = jnp.zeros(tables_in.shape[1:], F32)
            for point in range(times * count):
                piece_in[point, slot] = jnp.zeros(piece_in.shape[2:], F32)
                if slot < 2:
                    edge_in[point, slot] = jnp.zeros(edge_in.shape[2:], F32)
            for point in range(2):
                for turn in range(2):
                    if slot < 2:
                        block_in[point, turn, slot] = jnp.zeros(block_in.shape[3:], F32)
                        force_in[point, turn, slot] = jnp.zeros(force_in.shape[3:], F32)
                    else:
                        strip_in[point, turn, slot - 2] = jnp.zeros(strip_in.shape[3:], F32)


    pairs = (
        (ids_hbm, ids_ref),
        (walls_hbm, walls_ref),
        (scales_hbm, scales_ref),
        (guess_hbm, guess_ref),
        (faces_hbm, faces_ref),
        (volume_hbm, volume_ref),
        (init_hbm, init_ref),
        (forcing_hbm, forcing_ref),
    )
    loads = [pltpu.make_async_copy(a, b, load_sem.at[i]) for i, (a, b) in enumerate(pairs)]
    for copy in loads:
        copy.start()

    barrier = pltpu.get_barrier_semaphore()
    for slot in range(4):

        @pl.when(sent[slot])
        def _():
            pl.semaphore_signal(barrier, inc=1, device_id=(tme, around[slot]), device_id_type=MESH)

    for step in range(1, times):
        pl.semaphore_signal(
            barrier, inc=1, device_id=(lax.rem(tme + step, times), sme), device_id_type=MESH
        )

    def rows_of(layer, number=1):
        return pl.ds(layer * LAYER, number * LAYER)

    for copy in loads[:3]:
        copy.wait()
    local = ids_ref[...].reshape(1, own) - sme * own
    tables_out[0:6, :] = (1 - walls_ref[...]).astype(F32)
    tables_out[6:7, :] = scales_ref[...].reshape(1, own)
    tables_out[7:8, :] = local.astype(F32)
    perm = one_hot(local, 0, own)
    perm_ref[...] = perm

    def permuted_pair(first, second):
        return doubled(select_rows(perm_ref[...], jnp.concatenate([first, second], axis=0)))

    loads[3].wait()
    one, two = permuted_pair(guess_ref[0], guess_ref[1])
    guess_grid[0] = one
    guess_grid[1] = two
    exts[1, rows_of(off, layers), :] = one

    def pack(target, source, first, number):
        for layer in range(number):
            target[layer * LAYER : (layer + 1) * LAYER, :] = jnp.where(
                left_lanes(LAYER),
                source[rows_of(first + layer), :],
                source[rows_of(first + number + layer), :],
            )

    def unpack(source, target, first, number):
        for layer in range(number):
            one, two = doubled(source[layer * LAYER : (layer + 1) * LAYER, :])
            target[rows_of(first + layer), :] = one
            target[rows_of(first + number + layer), :] = two

    half = HALO // 2

    def remote(source, target, send, recv, slot):
        return pltpu.make_async_remote_copy(
            src_ref=source,
            dst_ref=target,
            send_sem=send,
            recv_sem=recv,
            device_id=(tme, around[slot]),
            device_id_type=MESH,
        )

    def state_copies(point, turn):
        copies = [
            (side, remote(
                block_out.at[point, turn],
                block_in.at[point, turn, side],
                block_send.at[point, turn, side],
                block_recv.at[point, turn, side],
                side,
            ))
            for side in range(2)
        ]
        return copies + [
            (2 + side, remote(
                strip_out.at[point, turn, side],
                strip_in.at[point, turn, side],
                strip_send.at[point, turn, side],
                strip_recv.at[point, turn, side],
                2 + side,
            ))
            for side in range(2)
        ]

    def send_state(point, turn):
        ext = exts.at[point]
        pack(block_out.at[point, turn], ext, off, layers // 2)
        pack(strip_out.at[point, turn, 0], ext, end - 2, 1)
        pack(strip_out.at[point, turn, 1], ext, off, 1)
        start(state_copies(point, turn))

    def receive_state(point, turn):
        ext = exts.at[point]
        arrive(state_copies(point, turn))
        unpack(block_in.at[point, turn, 0], ext, off - layers, layers // 2)
        unpack(block_in.at[point, turn, 1], ext, end, layers // 2)
        unpack(strip_in.at[point, turn, 0], ext, off - layers - 2, 1)
        unpack(strip_in.at[point, turn, 1], ext, end + layers, 1)

    def force_copies(point, turn):
        return [
            (side, remote(
                force_out.at[point, turn, side],
                force_in.at[point, turn, side],
                force_send.at[point, turn, side],
                force_recv.at[point, turn, side],
                side,
            ))
            for side in range(2)
        ]

    def send_force(point, turn):
        source = sources.at[point, 2 * turn]
        pack(force_out.at[point, turn, 0], source, layers - HALO, half)
        pack(force_out.at[point, turn, 1], source, 0, half)
        start(force_copies(point, turn))

    def add_force(point, turn):
        ext = exts.at[point]
        arrive(force_copies(point, turn))
        for side, first in enumerate((off - HALO, end)):
            for layer in range(half):
                one, two = doubled(force_in[point, turn, side, layer * LAYER : (layer + 1) * LAYER, :])
                ext[rows_of(first + layer), :] = ext[rows_of(first + layer), :] + one
                ext[rows_of(first + half + layer), :] = ext[rows_of(first + half + layer), :] + two

    for copy in loads[4:7]:
        copy.wait()

    @pl.when(tme == 0)
    def _():
        one, _ = permuted_pair(init_ref[...], init_ref[...])
        exts[0, rows_of(off, layers), :] = one

    pl.semaphore_wait(barrier, times - 1 + sum(here.astype(jnp.int32) for here in heard))

    guess_copy = pltpu.make_async_remote_copy(
        src_ref=guess_ref.at[count - 1],
        dst_ref=guess_in,
        send_sem=guess_send,
        recv_sem=guess_recv,
        device_id=(lax.rem(tme + 1, times), sme),
        device_id_type=MESH,
    )
    guess_copy.start()
    tables_copies = [
        (slot, remote(tables_out, tables_in.at[slot], tables_send.at[slot], tables_recv.at[slot], slot))
        for slot in range(4)
    ]
    start(tables_copies)

    @pl.when(tme == 0)
    def _():
        send_state(0, 0)

    send_state(1, 0)
    loads[7].wait()
    for step in (0, 2, 1, 3):
        one, two = permuted_pair(forcing_ref[step], forcing_ref[COARSEN + step])
        sources[0, step] = one
        sources[1, step] = two
        if step == 0:
            send_force(0, 0)
            send_force(1, 0)

    blocks = []
    for m in range(3):
        face = faces_ref[m]
        blocks.append(face.T)
        blocks.append(-face)
    blocks.append(volume_ref[...].T)
    blocks.append(jnp.zeros((DOF, DOF), F32))
    for pair in range(4):
        high, low = halves(jnp.concatenate(blocks[2 * pair : 2 * pair + 2], axis=1))
        weights[:, pair * 2 * DOF : (pair + 1) * 2 * DOF] = jnp.concatenate(
            [high, high, low, low], axis=0
        )

    def fill_table(first, number, hot, faces):
        flags, scale = table_of(hot, faces)
        table[rows_of(first, number), 0 : 6 * DOF] = flags
        table[rows_of(first, number), 6 * DOF : 8 * DOF] = scale

    fill_table(off - 1, layers, perm, tables_out[...])
    reach = 2 * HALO - 1 - layers
    spans = (
        (off - 1 - layers, 0, layers),
        (end - 1, 0, layers),
        (0, layers - reach, reach),
        (end - 1 + layers, 0, reach),
    )
    for slot, (place, begin, number) in enumerate(spans):
        arrive(tables_copies[slot : slot + 1])
        faces = tables_in[slot]
        hot = one_hot(faces[7:8].astype(jnp.int32), begin * LAYER, number * LAYER)
        fill_table(place, number, hot, faces)

    guess_copy.wait_recv()

    @pl.when(tme > 0)
    def _():
        one, _ = permuted_pair(guess_in[...], guess_in[...])
        exts[0, rows_of(off, layers), :] = one
        send_state(0, 0)

    send_force(1, 1)
    send_force(0, 1)

    def split_of(value):
        low = value - value.astype(BF16).astype(F32)
        return jnp.where(left_lanes(LAYER), value, low).astype(BF16)

    def products(blocks, part):
        rows = jnp.concatenate(blocks, axis=0)
        result = jnp.dot(
            jnp.concatenate([rows, rows], axis=1),
            weights[:, part * 4 * DOF : (part + 1) * 4 * DOF],
            preferred_element_type=F32,
        )
        return [result[i * LAYER : (i + 1) * LAYER] for i in range(len(blocks))]

    def combined(layer, flat, tall, below, above):
        left = left_lanes(LAYER)
        left3 = left.reshape(LAYER // GX, GX, 2 * DOF)
        px = flat[:, : 2 * DOF].reshape(LAYER // GX, GX, 2 * DOF)
        xs = jnp.where(left3, pltpu.roll(px, GX - 1, 1), pltpu.roll(px, 1, 1))
        py = flat[:, 2 * DOF :].reshape(LAYER // GX, GX, 2 * DOF)
        ys = jnp.where(
            left3,
            jnp.concatenate([py[1:], py[:1]], axis=0),
            jnp.concatenate([py[-1:], py[:-1]], axis=0),
        )
        zs = jnp.where(left, above[:, : 2 * DOF], below[:, : 2 * DOF])
        tab = slice((layer - 1) * LAYER, layer * LAYER)
        total = (
            table[tab, 0 : 2 * DOF] * xs.reshape(LAYER, 2 * DOF)
            + table[tab, 2 * DOF : 4 * DOF] * ys.reshape(LAYER, 2 * DOF)
        ) + (
            table[tab, 4 * DOF : 6 * DOF] * zs
            + table[tab, 6 * DOF : 8 * DOF] * tall[:, 2 * DOF :]
        )
        return total + swapped(total)

    def here(layer):
        return slice(layer * LAYER, (layer + 1) * LAYER)

    def advance(x, size, stage, layers_, flat, tall, finish):
        blocks = {}
        for layer in layers_:
            value = x[here(layer), :] + size / (4 - stage) * combined(
                layer, flat[layer], tall[layer], tall[layer - 1], tall[layer + 1]
            )
            if stage < 3:
                blocks[layer] = split_of(value)
            else:
                finish(layer, value)
        return blocks

    top = end + 2 * HALO

    def whole_step(x, size, low, high, finish, keep=False):
        blocks = {layer: split_of(x[here(layer), :]) for layer in range(low, high)}
        for stage in range(4):
            span = range(low + stage, high - stage)
            inner = span[1:-1]
            tall = dict(zip(span, products([blocks[layer] for layer in span], 1)))
            flat = dict(zip(inner, products([blocks[layer] for layer in inner], 0)))
            if keep:
                split[stage, 0] = blocks[span[0]]
                split[stage, 1] = blocks[span[-1]]
                for place, layer in enumerate((span[0], span[1], span[-1], span[-2])):
                    prod[stage, place] = tall[layer]
            blocks = advance(x, size, stage, inner, flat, tall, finish)

    def inner_step(x, size, finish, keep=True):
        whole_step(x, size, off - HALO, end + HALO, finish, keep)

    def outer_step(x, size, finish):
        lower = {layer: split_of(x[here(layer), :]) for layer in range(HALO)}
        upper = {layer: split_of(x[here(layer), :]) for layer in range(top - HALO, top)}
        for stage in range(4):
            sides = []
            for side, blocks in enumerate((lower, upper)):
                first = stage if side == 0 else top - stage - HALO
                span = range(first, first + HALO)
                next_in = first + HALO if side == 0 else first - 1
                second_in = next_in + 1 if side == 0 else next_in - 1
                tall = dict(zip(span, products([blocks[layer] for layer in span], 1)))
                tall[next_in] = prod[stage, 2 * side]
                tall[second_in] = prod[stage, 2 * side + 1]
                blocks[next_in] = split[stage, side]
                inner = range(first + 1, first + 1 + HALO) if side == 0 else range(first - 1, first - 1 + HALO)
                flat = dict(zip(inner, products([blocks[layer] for layer in inner], 0)))
                sides.append((inner, flat, tall))
            lower, upper = [
                advance(x, size, stage, inner, flat, tall, finish) for inner, flat, tall in sides
            ]

    def residual_copies(index):
        point = count * tme + index
        result = []
        for step in range(times - 1, 0, -1):
            result.append((
                step,
                pltpu.make_async_remote_copy(
                    src_ref=res_out.at[index],
                    dst_ref=res_in.at[point],
                    send_sem=res_send.at[index, step],
                    recv_sem=res_recv.at[point],
                    device_id=(lax.rem(tme + step, times), sme),
                    device_id_type=MESH,
                ),
            ))
        return result

    def fine(index, carry):
        turn = index // 2
        point = lax.rem(index + jnp.minimum(tme, 1), 2)
        ext = exts.at[point]
        receive_state(point, turn)

        def finish(step):
            def store(layer, value):
                if off <= layer < end:
                    value = value + sources[point, 2 * turn + step, rows_of(layer - off), :]
                ext[rows_of(layer), :] = value

            return store

        whole_step(ext, 1.0, off - 2 * HALO, end + 2 * HALO, finish(0))
        add_force(point, turn)
        inner_step(ext, 1.0, finish(1), keep=False)

        @pl.when(turn == 0)
        def _():
            send_state(point, 1)

        @pl.when(turn == 1)
        def _():
            place = count * tme + point
            errors[place] = ext[rows_of(off, layers), :] - guess_grid[point]
            pack(res_out.at[point], errors.at[place], 0, layers // 2)
            for distance, copy in residual_copies(point):

                @pl.when(tme + distance < times)
                def _():
                    copy.start()

        return carry

    lax.fori_loop(0, 4, fine, 0)

    final = count * tme + count - 1

    def take_residual(point):
        @pl.when(point < count * tme)
        def _():
            pltpu.make_async_remote_copy(
                src_ref=res_out.at[0],
                dst_ref=res_in.at[point],
                send_sem=res_send.at[0, 0],
                recv_sem=res_recv.at[point],
                device_id=(lax.rem(tme + 1, times), sme),
                device_id_type=MESH,
            ).wait_recv()
            unpack(res_in.at[point], errors.at[point], 0, layers // 2)

    def edge_copies(point):
        return [
            (side, remote(
                edge_out.at[point, side],
                edge_in.at[point, side],
                edge_send.at[point, side],
                edge_recv.at[point, side],
                side,
            ))
            for side in range(2)
        ]

    def send_edges(point):
        pack(edge_out.at[point, 0], errors.at[point], layers - HALO, half)
        pack(edge_out.at[point, 1], errors.at[point], 0, half)
        start(edge_copies(point))

    def piece_copies(point):
        return [
            (slot, remote(
                piece_out.at[point, (0, 1, 1, 0)[slot]],
                piece_in.at[point, slot],
                piece_send.at[point, slot],
                piece_recv.at[point, slot],
                slot,
            ))
            for slot in range(4)
        ]

    def send_pieces(point):
        pack(piece_out.at[point, 0], ext_a, off, 1)
        pack(piece_out.at[point, 1], ext_a, end - 2, 1)
        start(piece_copies(point))

    def receive_pieces(point):
        places = (off - layers, end + layers - 2, 0, end + layers)
        arrive(piece_copies(point))
        for slot in range(4):
            unpack(piece_in.at[point, slot], ext_a, places[slot], 1)

    def receive_edges(point, place):
        arrive(edge_copies(point))
        for side in range(2):
            place(side, edge_in.at[point, side])

    def pass_residual(point):
        @pl.when(point <= final)
        def _():
            take_residual(point)

        @pl.when(point < final)
        def _():
            send_edges(point)

    pass_residual(0)
    ext_a[rows_of(off, layers), :] = errors[0]

    @pl.when(final > 1)
    def _():
        send_pieces(0)

    pass_residual(1)
    pass_residual(2)

    receive_edges(0, lambda side, ref: unpack(ref, ext_a, off - HALO if side == 0 else end, half))

    def coarse(point, carry):
        def finish(layer, value):
            inside = rows_of(layer - off)
            value = value + errors[point, inside, :]
            ext_a[rows_of(layer), :] = value
            errors[point, inside, :] = value

        inner_step(ext_a, float(COARSEN), finish)

        @pl.when(point < final - 1)
        def _():
            send_pieces(point)

        pass_residual(point + 2)

        @pl.when(point < final)
        def _():
            receive_pieces(point - 1)
            receive_edges(
                point, lambda side, ref: unpack(ref, spare, off - HALO if side == 0 else end, half)
            )

            def finish_outer(layer, value):
                ext_a[rows_of(layer), :] = value + spare[rows_of(layer), :]

            outer_step(ext_a, float(COARSEN), finish_outer)

        return carry

    lax.fori_loop(1, final + 1, coarse, 0)

    packed = jnp.where(left_lanes(own), errors[final - 1], errors[final])
    parts = [
        lax.dot_general(part, perm_ref[...], (((0,), (0,)), ((), ())), preferred_element_type=F32)
        for part in thirds(packed)
    ]
    result = (parts[0] + parts[1]) + parts[2]
    out_ref[0] = result[:DOF]
    out_ref[1] = result[DOF:]

    guess_copy.wait_send()
    finish_sends(tables_copies)

    for point in range(2):
        for turn in range(2):
            finish_sends(state_copies(point, turn) + force_copies(point, turn))
    for index in range(2):
        for distance, copy in residual_copies(index):

            @pl.when(tme + distance < times)
            def _():
                copy.wait_send()

    def sweep_done(point, carry):
        finish_sends(edge_copies(point))

        @pl.when(point < final - 1)
        def _():
            finish_sends(piece_copies(point))

        return carry

    lax.fori_loop(0, final, sweep_done, 0)


def body(init_state, guess, forcing, volume_block, face_blocks, elem_scales, element_ids, neighbours, walls):
    own = element_ids.shape[0]
    layers = own // LAYER
    count = guess.shape[0]
    times = lax.axis_size("tm")
    points = times * count
    ext = (layers + 4 * HALO) * LAYER
    wide = 2 * DOF
    vmem = pltpu.VMEM
    dma = pltpu.SemaphoreType.DMA
    errors = pl.pallas_call(
        functools.partial(kernel, layers, count),
        out_shape=jax.ShapeDtypeStruct(guess.shape, F32),
        in_specs=[pl.BlockSpec(memory_space=pl.ANY)] * 8,
        out_specs=pl.BlockSpec(memory_space=pltpu.VMEM),
        scratch_shapes=[
            vmem(init_state.shape, F32),
            vmem(guess.shape, F32),
            vmem(forcing.shape, F32),
            vmem(volume_block.shape, F32),
            vmem(face_blocks.shape, F32),
            vmem((own,), F32),
            vmem((own,), jnp.int32),
            vmem(walls.shape, jnp.int32),
            vmem((4 * DOF, 8 * DOF), BF16),
            vmem((ext - 2 * LAYER, 8 * DOF), F32),
            vmem((own, own), BF16),
            vmem((2, COARSEN, own, wide), F32),
            vmem((2, own, wide), F32),
            vmem((2, ext, wide), F32),
            vmem((ext, wide), F32),
            vmem((4, 2, LAYER, wide), BF16),
            vmem((4, 4, LAYER, 4 * DOF), F32),
            vmem((points, own, wide), F32),
            vmem((8, own), F32),
            vmem((4, 8, own), F32),
            vmem((DOF, own), F32),
            vmem((2, 2, own // 2, wide), F32),
            vmem((2, 2, 2, own // 2, wide), F32),
            vmem((2, 2, 2, LAYER, wide), F32),
            vmem((2, 2, 2, LAYER, wide), F32),
            vmem((2, 2, 2, HALO // 2 * LAYER, wide), F32),
            vmem((2, 2, 2, HALO // 2 * LAYER, wide), F32),
            vmem((points, 2, LAYER, wide), F32),
            vmem((points, 4, LAYER, wide), F32),
            vmem((points, 2, HALO // 2 * LAYER, wide), F32),
            vmem((points, 2, HALO // 2 * LAYER, wide), F32),
            vmem((2, own // 2, wide), F32),
            vmem((points, own // 2, wide), F32),
            dma((8,)),
            dma((4,)),
            dma((4,)),
            dma,
            dma,
            dma((2, 2, 2)),
            dma((2, 2, 2)),
            dma((2, 2, 2)),
            dma((2, 2, 2)),
            dma((2, 2, 2)),
            dma((2, 2, 2)),
            dma((points, 4)),
            dma((points, 4)),
            dma((points, 2)),
            dma((points, 2)),
            dma((2, times)),
            dma((points,)),
        ],
        compiler_params=pltpu.CompilerParams(
            collective_id=0, has_side_effects=True, vmem_limit_bytes=56 * 1024 * 1024
        ),
    )(
        init_state,
        guess,
        forcing,
        volume_block,
        face_blocks,
        elem_scales,
        element_ids,
        walls,
    )
    return guess + errors


def solution(mesh):
    return jax.shard_map(
        body,
        mesh=mesh,
        in_specs=(
            P(None, "space"),
            P("tm", None, "space"),
            P("tm", None, "space"),
            P(),
            P(),
            P("space"),
            P("space"),
            P(None, "space"),
            P(None, "space"),
        ),
        out_specs=P("tm", None, "space"),
        check_vma=False,
    )
```

```python
import functools
import jax
import jax.numpy as jnp
from jax import lax
from jax.experimental import pallas as pl
from jax.experimental.pallas import tpu as pltpu
from jax.sharding import PartitionSpec as P

GX = 8
LAYER = 64
DOF = 64
COARSEN = 4
HALO = 4
MESH = pl.DeviceIdType.MESH
F32 = jnp.float32
BF16 = jnp.bfloat16


def halves(x):
    hi = x.astype(BF16)
    return hi, (x - hi.astype(F32)).astype(BF16)


def thirds(x):
    hi = x.astype(BF16)
    rest = x - hi.astype(F32)
    mid = rest.astype(BF16)
    return hi, mid, (rest - mid.astype(F32)).astype(BF16)


def times_t(a, b):
    return lax.dot_general(a, b, (((1,), (1,)), ((), ())), preferred_element_type=F32)


def select_rows(perm, values):
    hi, mid, lo = thirds(values)
    return (times_t(perm, hi) + times_t(perm, mid)) + times_t(perm, lo)


def left_lanes(rows):
    return lax.broadcasted_iota(jnp.int32, (rows, 2 * DOF), 1) < DOF


def swapped(x):
    return pltpu.roll(x, DOF, 1)


def doubled(packed):
    left = left_lanes(packed.shape[0])
    other = swapped(packed)
    return jnp.where(left, packed, other), jnp.where(left, other, packed)


def one_hot(ids_row, first, rows):
    cells = lax.broadcasted_iota(jnp.int32, (rows, ids_row.shape[1]), 0) + first
    return (ids_row == cells).astype(F32).astype(BF16)


def table_of(perm, faces):
    flags = jnp.concatenate(
        [jnp.broadcast_to(faces[f : f + 1], (DOF, faces.shape[1])) for f in range(6)], axis=0
    )
    scale = jnp.broadcast_to(faces[6:7], (2 * DOF, faces.shape[1]))
    return times_t(perm, flags.astype(BF16)), select_rows(perm, scale)


def kernel(
    layers,
    count,
    init_hbm,
    guess_hbm,
    forcing_hbm,
    volume_hbm,
    faces_hbm,
    scales_hbm,
    ids_hbm,
    walls_hbm,
    out_ref,
    init_ref,
    guess_ref,
    forcing_ref,
    volume_ref,
    faces_ref,
    scales_ref,
    ids_ref,
    walls_ref,
    weights,
    table,
    perm_ref,
    sources,
    guess_grid,
    exts,
    ext_a,
    spare,
    split,
    prod,
    errors,
    tables_out,
    tables_in,
    guess_in,
    block_out,
    block_in,
    strip_out,
    strip_in,
    force_out,
    force_in,
    piece_out,
    piece_in,
    edge_out,
    edge_in,
    far_out,
    far_in,
    rest_out,
    rest_in,
    load_sem,
    tables_send,
    tables_recv,
    guess_send,
    guess_recv,
    block_send,
    block_recv,
    strip_send,
    strip_recv,
    force_send,
    force_recv,
    piece_send,
    piece_recv,
    edge_send,
    edge_recv,
    far_send,
    far_recv,
    rest_send,
    rest_recv,
):
    times = lax.axis_size("tm")
    spaces = lax.axis_size("space")
    tme = lax.axis_index("tm")
    sme = lax.axis_index("space")
    own = layers * LAYER
    off = 2 * HALO
    end = off + layers
    around = [lax.rem(sme + spaces + step, spaces) for step in (1, -1, 2, -2)]
    heard = [sme >= 1, sme <= spaces - 2, sme >= 2, sme <= spaces - 3]
    sent = [heard[1], heard[0], heard[3], heard[2]]

    def start(copies):
        for slot, copy in copies:
            pl.when(sent[slot])(copy.start)

    def arrive(copies):
        for slot, copy in copies:
            pl.when(heard[slot])(copy.wait_recv)

    def finish_sends(copies):
        for slot, copy in copies:
            pl.when(sent[slot])(copy.wait_send)

    for slot in range(4):

        @pl.when(jnp.logical_not(heard[slot]))
        def _():
            tables_in[slot] = jnp.zeros(tables_in.shape[1:], F32)
            for point in range(times * count):
                piece_in[point, slot] = jnp.zeros(piece_in.shape[2:], F32)
                if slot < 2:
                    edge_in[point, slot] = jnp.zeros(edge_in.shape[2:], F32)
            for point in range(2):
                for turn in range(2):
                    if slot < 2:
                        block_in[point, turn, slot] = jnp.zeros(block_in.shape[3:], F32)
                        force_in[point, turn, slot] = jnp.zeros(force_in.shape[3:], F32)
                    else:
                        strip_in[point, turn, slot - 2] = jnp.zeros(strip_in.shape[3:], F32)


    pairs = (
        (ids_hbm, ids_ref),
        (walls_hbm, walls_ref),
        (scales_hbm, scales_ref),
        (guess_hbm, guess_ref),
        (faces_hbm, faces_ref),
        (volume_hbm, volume_ref),
        (init_hbm, init_ref),
        (forcing_hbm, forcing_ref),
    )
    loads = [pltpu.make_async_copy(a, b, load_sem.at[i]) for i, (a, b) in enumerate(pairs)]
    for copy in loads:
        copy.start()

    barrier = pltpu.get_barrier_semaphore()
    for slot in range(4):

        @pl.when(sent[slot])
        def _():
            pl.semaphore_signal(barrier, inc=1, device_id=(tme, around[slot]), device_id_type=MESH)

    for step in range(1, times):
        pl.semaphore_signal(
            barrier, inc=1, device_id=(lax.rem(tme + step, times), sme), device_id_type=MESH
        )

    def rows_of(layer, number=1):
        first = layer * LAYER
        if not isinstance(layer, int):
            first = pl.multiple_of(first, LAYER)
        return pl.ds(first, number * LAYER)

    for copy in loads[:3]:
        copy.wait()
    local = ids_ref[...].reshape(1, own) - sme * own
    tables_out[0:6, :] = (1 - walls_ref[...]).astype(F32)
    tables_out[6:7, :] = scales_ref[...].reshape(1, own)
    tables_out[7:8, :] = local.astype(F32)
    perm = one_hot(local, 0, own)
    perm_ref[...] = perm

    def permuted_pair(first, second):
        return doubled(select_rows(perm_ref[...], jnp.concatenate([first, second], axis=0)))

    loads[3].wait()
    one, two = permuted_pair(guess_ref[0], guess_ref[1])
    guess_grid[0] = one
    guess_grid[1] = two
    exts[1, rows_of(off, layers), :] = one

    def pack(target, source, first, number):
        for layer in range(number):
            target[layer * LAYER : (layer + 1) * LAYER, :] = jnp.where(
                left_lanes(LAYER),
                source[rows_of(first + layer), :],
                source[rows_of(first + number + layer), :],
            )

    def unpack(source, target, first, number):
        for layer in range(number):
            one, two = doubled(source[layer * LAYER : (layer + 1) * LAYER, :])
            target[rows_of(first + layer), :] = one
            target[rows_of(first + number + layer), :] = two

    half = HALO // 2

    def remote(source, target, send, recv, slot):
        return pltpu.make_async_remote_copy(
            src_ref=source,
            dst_ref=target,
            send_sem=send,
            recv_sem=recv,
            device_id=(tme, around[slot]),
            device_id_type=MESH,
        )

    def state_copies(point, turn):
        copies = [
            (side, remote(
                block_out.at[point, turn],
                block_in.at[point, turn, side],
                block_send.at[point, turn, side],
                block_recv.at[point, turn, side],
                side,
            ))
            for side in range(2)
        ]
        return copies + [
            (2 + side, remote(
                strip_out.at[point, turn, side],
                strip_in.at[point, turn, side],
                strip_send.at[point, turn, side],
                strip_recv.at[point, turn, side],
                2 + side,
            ))
            for side in range(2)
        ]

    def send_state(point, turn):
        ext = exts.at[point]
        pack(block_out.at[point, turn], ext, off, layers // 2)
        pack(strip_out.at[point, turn, 0], ext, end - 2, 1)
        pack(strip_out.at[point, turn, 1], ext, off, 1)
        start(state_copies(point, turn))

    def receive_state(point, turn):
        ext = exts.at[point]
        arrive(state_copies(point, turn))
        unpack(block_in.at[point, turn, 0], ext, off - layers, layers // 2)
        unpack(block_in.at[point, turn, 1], ext, end, layers // 2)
        unpack(strip_in.at[point, turn, 0], ext, off - layers - 2, 1)
        unpack(strip_in.at[point, turn, 1], ext, end + layers, 1)

    def force_copies(point, turn):
        return [
            (side, remote(
                force_out.at[point, turn, side],
                force_in.at[point, turn, side],
                force_send.at[point, turn, side],
                force_recv.at[point, turn, side],
                side,
            ))
            for side in range(2)
        ]

    def send_force(point, turn):
        source = sources.at[point, 2 * turn]
        pack(force_out.at[point, turn, 0], source, layers - HALO, half)
        pack(force_out.at[point, turn, 1], source, 0, half)
        start(force_copies(point, turn))

    def add_force(point, turn):
        ext = exts.at[point]
        arrive(force_copies(point, turn))
        for side, first in enumerate((off - HALO, end)):
            for layer in range(half):
                one, two = doubled(force_in[point, turn, side, layer * LAYER : (layer + 1) * LAYER, :])
                ext[rows_of(first + layer), :] = ext[rows_of(first + layer), :] + one
                ext[rows_of(first + half + layer), :] = ext[rows_of(first + half + layer), :] + two

    for copy in loads[4:7]:
        copy.wait()

    @pl.when(tme == 0)
    def _():
        one, _ = permuted_pair(init_ref[...], init_ref[...])
        exts[0, rows_of(off, layers), :] = one

    pl.semaphore_wait(barrier, times - 1 + sum(here.astype(jnp.int32) for here in heard))

    guess_copy = pltpu.make_async_remote_copy(
        src_ref=guess_ref.at[count - 1],
        dst_ref=guess_in,
        send_sem=guess_send,
        recv_sem=guess_recv,
        device_id=(lax.rem(tme + 1, times), sme),
        device_id_type=MESH,
    )
    guess_copy.start()
    tables_copies = [
        (slot, remote(tables_out, tables_in.at[slot], tables_send.at[slot], tables_recv.at[slot], slot))
        for slot in range(4)
    ]
    start(tables_copies)

    @pl.when(tme == 0)
    def _():
        send_state(0, 0)

    send_state(1, 0)
    loads[7].wait()
    for step in (0, 2, 1, 3):
        one, two = permuted_pair(forcing_ref[step], forcing_ref[COARSEN + step])
        sources[0, step] = one
        sources[1, step] = two
        if step == 0:
            send_force(0, 0)
            send_force(1, 0)

    blocks = []
    for m in range(3):
        face = faces_ref[m]
        blocks.append(face.T)
        blocks.append(-face)
    blocks.append(volume_ref[...].T)
    blocks.append(jnp.zeros((DOF, DOF), F32))
    for pair in range(4):
        high, low = halves(jnp.concatenate(blocks[2 * pair : 2 * pair + 2], axis=1))
        weights[:, pair * 2 * DOF : (pair + 1) * 2 * DOF] = jnp.concatenate(
            [high, high, low, low], axis=0
        )

    def fill_table(first, number, hot, faces):
        flags, scale = table_of(hot, faces)
        table[rows_of(first, number), 0 : 6 * DOF] = flags
        table[rows_of(first, number), 6 * DOF : 8 * DOF] = scale

    fill_table(off - 1, layers, perm, tables_out[...])
    reach = 2 * HALO - 1 - layers
    spans = (
        (off - 1 - layers, 0, layers),
        (end - 1, 0, layers),
        (0, layers - reach, reach),
        (end - 1 + layers, 0, reach),
    )
    for slot, (place, begin, number) in enumerate(spans):
        arrive(tables_copies[slot : slot + 1])
        faces = tables_in[slot]
        hot = one_hot(faces[7:8].astype(jnp.int32), begin * LAYER, number * LAYER)
        fill_table(place, number, hot, faces)

    guess_copy.wait_recv()

    @pl.when(tme > 0)
    def _():
        one, _ = permuted_pair(guess_in[...], guess_in[...])
        exts[0, rows_of(off, layers), :] = one
        send_state(0, 0)

    send_force(1, 1)
    send_force(0, 1)

    def split_of(value):
        low = value - value.astype(BF16).astype(F32)
        return jnp.where(left_lanes(LAYER), value, low).astype(BF16)

    def products(blocks, part):
        rows = jnp.concatenate(blocks, axis=0)
        result = jnp.dot(
            jnp.concatenate([rows, rows], axis=1),
            weights[:, part * 4 * DOF : (part + 1) * 4 * DOF],
            preferred_element_type=F32,
        )
        return [result[i * LAYER : (i + 1) * LAYER] for i in range(len(blocks))]

    def combined(layer, flat, tall, below, above):
        left = left_lanes(LAYER)
        left3 = left.reshape(LAYER // GX, GX, 2 * DOF)
        px = flat[:, : 2 * DOF].reshape(LAYER // GX, GX, 2 * DOF)
        xs = jnp.where(left3, pltpu.roll(px, GX - 1, 1), pltpu.roll(px, 1, 1))
        py = flat[:, 2 * DOF :].reshape(LAYER // GX, GX, 2 * DOF)
        ys = jnp.where(
            left3,
            jnp.concatenate([py[1:], py[:1]], axis=0),
            jnp.concatenate([py[-1:], py[:-1]], axis=0),
        )
        zs = jnp.where(left, above[:, : 2 * DOF], below[:, : 2 * DOF])
        tab = slice((layer - 1) * LAYER, layer * LAYER)
        total = (
            table[tab, 0 : 2 * DOF] * xs.reshape(LAYER, 2 * DOF)
            + table[tab, 2 * DOF : 4 * DOF] * ys.reshape(LAYER, 2 * DOF)
        ) + (
            table[tab, 4 * DOF : 6 * DOF] * zs
            + table[tab, 6 * DOF : 8 * DOF] * tall[:, 2 * DOF :]
        )
        return total + swapped(total)

    def here(layer):
        return slice(layer * LAYER, (layer + 1) * LAYER)

    def advance(x, size, stage, layers_, flat, tall, finish):
        blocks = {}
        for layer in layers_:
            value = x[here(layer), :] + size / (4 - stage) * combined(
                layer, flat[layer], tall[layer], tall[layer - 1], tall[layer + 1]
            )
            if stage < 3:
                blocks[layer] = split_of(value)
            else:
                finish(layer, value)
        return blocks

    top = end + 2 * HALO

    def whole_step(x, size, low, high, finish, keep=False):
        blocks = {layer: split_of(x[here(layer), :]) for layer in range(low, high)}
        for stage in range(4):
            span = range(low + stage, high - stage)
            inner = span[1:-1]
            tall = dict(zip(span, products([blocks[layer] for layer in span], 1)))
            flat = dict(zip(inner, products([blocks[layer] for layer in inner], 0)))
            if keep:
                split[stage, 0] = blocks[span[0]]
                split[stage, 1] = blocks[span[-1]]
                for place, layer in enumerate((span[0], span[1], span[-1], span[-2])):
                    prod[stage, place] = tall[layer]
            blocks = advance(x, size, stage, inner, flat, tall, finish)

    def inner_step(x, size, finish, keep=True):
        whole_step(x, size, off - HALO, end + HALO, finish, keep)

    def outer_step(x, size, finish):
        blocks = {
            layer: split_of(x[here(layer), :])
            for layer in (*range(HALO), *range(top - HALO, top))
        }
        for stage in range(4):
            low, high = stage, top - stage - HALO
            span = (*range(low, low + HALO), *range(high, high + HALO))
            inner = (*range(low + 1, low + 1 + HALO), *range(high - 1, high - 1 + HALO))
            tall = dict(zip(span, products([blocks[layer] for layer in span], 1)))
            for place, layer in enumerate((low + HALO, low + HALO + 1, high - 1, high - 2)):
                tall[layer] = prod[stage, place]
            blocks[low + HALO] = split[stage, 0]
            blocks[high - 1] = split[stage, 1]
            flat = dict(zip(inner, products([blocks[layer] for layer in inner], 0)))
            blocks = advance(x, size, stage, inner, flat, tall, finish)

    core = lax.rem(sme, 2)
    far_first = core * (layers - HALO)
    rest_first = (1 - core) * HALO

    def residual_copies(index):
        point = count * tme + index
        result = []
        for step in range(times - 1, 0, -1):
            for source, target, send, recv in (
                (far_out, far_in, far_send, far_recv),
                (rest_out, rest_in, rest_send, rest_recv),
            ):
                result.append((
                    step,
                    pltpu.make_async_remote_copy(
                        src_ref=source.at[index],
                        dst_ref=target.at[point],
                        send_sem=send.at[index, step],
                        recv_sem=recv.at[point],
                        device_id=(lax.rem(tme + step, times), sme),
                        device_id_type=MESH,
                    ),
                ))
        return result

    final = count * tme + count - 1

    def edge_copies(point):
        return [
            (side, remote(
                edge_out.at[point, side],
                edge_in.at[point, side],
                edge_send.at[point, side],
                edge_recv.at[point, side],
                side,
            ))
            for side in range(2)
        ]

    def send_edge(point, side):
        pack(edge_out.at[point, side], errors.at[point], layers - HALO if side == 0 else 0, half)
        start(edge_copies(point)[side : side + 1])

    def landed(source, target, send, recv, point):
        pltpu.make_async_remote_copy(
            src_ref=source.at[0],
            dst_ref=target.at[point],
            send_sem=send.at[0, 0],
            recv_sem=recv.at[point],
            device_id=(lax.rem(tme + 1, times), sme),
            device_id_type=MESH,
        ).wait_recv()

    def piece_copies(point):
        return [
            (slot, remote(
                piece_out.at[point, (0, 1, 1, 0)[slot]],
                piece_in.at[point, slot],
                piece_send.at[point, slot],
                piece_recv.at[point, slot],
                slot,
            ))
            for slot in range(4)
        ]

    def send_pieces(point):
        pack(piece_out.at[point, 0], ext_a, off, 1)
        pack(piece_out.at[point, 1], ext_a, end - 2, 1)
        start(piece_copies(point))

    def receive_pieces(point):
        places = (off - layers, end + layers - 2, 0, end + layers)
        arrive(piece_copies(point))
        for slot in range(4):
            unpack(piece_in.at[point, slot], ext_a, places[slot], 1)

    def receive_edges(point, place):
        arrive(edge_copies(point))
        for side in range(2):
            place(side, edge_in.at[point, side])

    def pass_residual(point):
        passed = point < final
        foreign = point < count * tme

        @pl.when(jnp.logical_and(point <= final, foreign))
        def _():
            landed(far_out, far_in, far_send, far_recv, point)
            for side in range(2):

                @pl.when(jnp.logical_and(passed, core == 1 - side))
                def _():
                    start([(side, remote(
                        far_in.at[point],
                        edge_in.at[point, side],
                        edge_send.at[point, side],
                        edge_recv.at[point, side],
                        side,
                    ))])

            landed(rest_out, rest_in, rest_send, rest_recv, point)
            unpack(far_in.at[point], errors.at[point], far_first, half)
            unpack(rest_in.at[point], errors.at[point], rest_first, 1)
            for side in range(2):

                @pl.when(jnp.logical_and(passed, core == side))
                def _():
                    send_edge(point, side)

        @pl.when(jnp.logical_and(passed, jnp.logical_not(foreign)))
        def _():
            for side in range(2):
                send_edge(point, side)

    def begin_sweep():
        pass_residual(0)
        ext_a[rows_of(off, layers), :] = errors[0]

        @pl.when(final > 1)
        def _():
            send_pieces(0)

    def fine(index, carry):
        @pl.when(jnp.logical_and(index == 3, tme == times - 1))
        def _():
            begin_sweep()

        turn = index // 2
        point = lax.rem(index + jnp.minimum(tme, 1), 2)
        ext = exts.at[point]
        receive_state(point, turn)

        def finish(step):
            def store(layer, value):
                if off <= layer < end:
                    value = value + sources[point, 2 * turn + step, rows_of(layer - off), :]
                ext[rows_of(layer), :] = value

            return store

        whole_step(ext, 1.0, off - 2 * HALO, end + 2 * HALO, finish(0))
        add_force(point, turn)
        inner_step(ext, 1.0, finish(1), keep=False)

        @pl.when(turn == 0)
        def _():
            send_state(point, 1)

        @pl.when(turn == 1)
        def _():
            place = count * tme + point
            errors[place] = ext[rows_of(off, layers), :] - guess_grid[point]
            pack(far_out.at[point], errors.at[place], far_first, half)
            pack(rest_out.at[point], errors.at[place], rest_first, 1)
            for distance, copy in residual_copies(point):

                @pl.when(tme + distance < times)
                def _():
                    copy.start()

        return carry

    lax.fori_loop(0, 4, fine, 0)

    @pl.when(tme < times - 1)
    def _():
        begin_sweep()

    pass_residual(1)

    receive_edges(0, lambda side, ref: unpack(ref, ext_a, off - HALO if side == 0 else end, half))

    def coarse(point, carry):
        def finish(layer, value):
            inside = rows_of(layer - off)
            value = value + errors[point, inside, :]
            ext_a[rows_of(layer), :] = value
            errors[point, inside, :] = value

        inner_step(ext_a, float(COARSEN), finish)

        @pl.when(point < final - 1)
        def _():
            send_pieces(point)

        @pl.when(point == 1)
        def _():
            pass_residual(2)

        pass_residual(point + 2)

        @pl.when(point < final)
        def _():
            receive_edges(
                point, lambda side, ref: unpack(ref, spare, off - HALO if side == 0 else end, half)
            )
            receive_pieces(point - 1)

            def finish_outer(layer, value):
                ext_a[rows_of(layer), :] = value + spare[rows_of(layer), :]

            outer_step(ext_a, float(COARSEN), finish_outer)

        return carry

    lax.fori_loop(1, final + 1, coarse, 0)

    packed = jnp.where(left_lanes(own), errors[final - 1], errors[final])
    parts = [
        lax.dot_general(part, perm_ref[...], (((0,), (0,)), ((), ())), preferred_element_type=F32)
        for part in halves(packed)
    ]
    result = parts[0] + parts[1]
    out_ref[0] = result[:DOF]
    out_ref[1] = result[DOF:]

    guess_copy.wait_send()
    finish_sends(tables_copies)

    for point in range(2):
        for turn in range(2):
            finish_sends(state_copies(point, turn) + force_copies(point, turn))
    for index in range(2):
        for distance, copy in residual_copies(index):

            @pl.when(tme + distance < times)
            def _():
                copy.wait_send()

    def sweep_done(point, carry):
        finish_sends(edge_copies(point))

        @pl.when(point < final - 1)
        def _():
            finish_sends(piece_copies(point))

        return carry

    lax.fori_loop(0, final, sweep_done, 0)


def body(init_state, guess, forcing, volume_block, face_blocks, elem_scales, element_ids, neighbours, walls):
    own = element_ids.shape[0]
    layers = own // LAYER
    count = guess.shape[0]
    times = lax.axis_size("tm")
    points = times * count
    ext = (layers + 4 * HALO) * LAYER
    wide = 2 * DOF
    vmem = pltpu.VMEM
    dma = pltpu.SemaphoreType.DMA
    errors = pl.pallas_call(
        functools.partial(kernel, layers, count),
        out_shape=jax.ShapeDtypeStruct(guess.shape, F32),
        in_specs=[pl.BlockSpec(memory_space=pl.ANY)] * 8,
        out_specs=pl.BlockSpec(memory_space=pltpu.VMEM),
        scratch_shapes=[
            vmem(init_state.shape, F32),
            vmem(guess.shape, F32),
            vmem(forcing.shape, F32),
            vmem(volume_block.shape, F32),
            vmem(face_blocks.shape, F32),
            vmem((own,), F32),
            vmem((own,), jnp.int32),
            vmem(walls.shape, jnp.int32),
            vmem((4 * DOF, 8 * DOF), BF16),
            vmem((ext - 2 * LAYER, 8 * DOF), F32),
            vmem((own, own), BF16),
            vmem((2, COARSEN, own, wide), F32),
            vmem((2, own, wide), F32),
            vmem((2, ext, wide), F32),
            vmem((ext, wide), F32),
            vmem((ext, wide), F32),
            vmem((4, 2, LAYER, wide), BF16),
            vmem((4, 4, LAYER, 4 * DOF), F32),
            vmem((points, own, wide), F32),
            vmem((8, own), F32),
            vmem((4, 8, own), F32),
            vmem((DOF, own), F32),
            vmem((2, 2, own // 2, wide), F32),
            vmem((2, 2, 2, own // 2, wide), F32),
            vmem((2, 2, 2, LAYER, wide), F32),
            vmem((2, 2, 2, LAYER, wide), F32),
            vmem((2, 2, 2, HALO // 2 * LAYER, wide), F32),
            vmem((2, 2, 2, HALO // 2 * LAYER, wide), F32),
            vmem((points, 2, LAYER, wide), F32),
            vmem((points, 4, LAYER, wide), F32),
            vmem((points, 2, HALO // 2 * LAYER, wide), F32),
            vmem((points, 2, HALO // 2 * LAYER, wide), F32),
            vmem((2, HALO // 2 * LAYER, wide), F32),
            vmem((points, HALO // 2 * LAYER, wide), F32),
            vmem((2, LAYER, wide), F32),
            vmem((points, LAYER, wide), F32),
            dma((8,)),
            dma((4,)),
            dma((4,)),
            dma,
            dma,
            dma((2, 2, 2)),
            dma((2, 2, 2)),
            dma((2, 2, 2)),
            dma((2, 2, 2)),
            dma((2, 2, 2)),
            dma((2, 2, 2)),
            dma((points, 4)),
            dma((points, 4)),
            dma((points, 2)),
            dma((points, 2)),
            dma((2, times)),
            dma((points,)),
            dma((2, times)),
            dma((points,)),
        ],
        compiler_params=pltpu.CompilerParams(
            collective_id=0, has_side_effects=True, vmem_limit_bytes=40 * 1024 * 1024
        ),
    )(
        *(
            pltpu.with_memory_space_constraint(field, pltpu.HBM)
            for field in (
                init_state,
                guess,
                forcing,
                volume_block,
                face_blocks,
                elem_scales,
                element_ids,
                walls,
            )
        )
    )
    return guess + errors


def solution(mesh):
    return jax.shard_map(
        body,
        mesh=mesh,
        in_specs=(
            P(None, "space"),
            P("tm", None, "space"),
            P("tm", None, "space"),
            P(),
            P(),
            P("space"),
            P("space"),
            P(None, "space"),
            P(None, "space"),
        ),
        out_specs=P("tm", None, "space"),
        check_vma=False,
    )
```

```python
import functools
import jax
import jax.numpy as jnp
from jax import lax
from jax.experimental import pallas as pl
from jax.experimental.pallas import tpu as pltpu
from jax.sharding import PartitionSpec as P

GX = 8
LAYER = 64
DOF = 64
COARSEN = 4
HALO = 4
MESH = pl.DeviceIdType.MESH
F32 = jnp.float32
BF16 = jnp.bfloat16


def halves(x):
    hi = x.astype(BF16)
    return hi, (x - hi.astype(F32)).astype(BF16)


def thirds(x):
    hi = x.astype(BF16)
    rest = x - hi.astype(F32)
    mid = rest.astype(BF16)
    return hi, mid, (rest - mid.astype(F32)).astype(BF16)


def times_t(a, b):
    return lax.dot_general(a, b, (((1,), (1,)), ((), ())), preferred_element_type=F32)


def select_rows(perm, values):
    hi, mid, lo = thirds(values)
    return (times_t(perm, hi) + times_t(perm, mid)) + times_t(perm, lo)


def select_rows_16(perm, values):
    high, low = halves(values)
    return times_t(perm, high) + times_t(perm, low)


def left_lanes(rows):
    return lax.broadcasted_iota(jnp.int32, (rows, 2 * DOF), 1) < DOF


def swapped(x):
    return pltpu.roll(x, DOF, 1)


def doubled(packed):
    left = left_lanes(packed.shape[0])
    other = swapped(packed)
    return jnp.where(left, packed, other), jnp.where(left, other, packed)


def one_hot(ids_row, first, rows):
    cells = lax.broadcasted_iota(jnp.int32, (rows, ids_row.shape[1]), 0) + first
    return (ids_row == cells).astype(F32).astype(BF16)


def table_of(perm, faces):
    flags = jnp.concatenate(
        [jnp.broadcast_to(faces[f : f + 1], (DOF, faces.shape[1])) for f in range(6)], axis=0
    )
    scale = jnp.broadcast_to(faces[6:7], (2 * DOF, faces.shape[1]))
    return times_t(perm, flags.astype(BF16)), select_rows(perm, scale)


def kernel(
    layers,
    count,
    init_hbm,
    guess_hbm,
    forcing_hbm,
    volume_hbm,
    faces_hbm,
    scales_hbm,
    ids_hbm,
    walls_hbm,
    out_ref,
    init_ref,
    guess_ref,
    forcing_ref,
    volume_ref,
    faces_ref,
    scales_ref,
    ids_ref,
    walls_ref,
    weights,
    table,
    perm_ref,
    sources,
    guess_grid,
    exts,
    ext_a,
    split,
    prod,
    errors,
    tables_out,
    tables_in,
    guess_in,
    block_out,
    block_in,
    strip_out,
    strip_in,
    force_out,
    force_in,
    piece_out,
    piece_in,
    edge_out,
    edge_in,
    far_out,
    far_in,
    rest_out,
    rest_in,
    load_sem,
    tables_send,
    tables_recv,
    guess_send,
    guess_recv,
    block_send,
    block_recv,
    strip_send,
    strip_recv,
    force_send,
    force_recv,
    piece_send,
    piece_recv,
    edge_send,
    edge_recv,
    far_send,
    far_recv,
    rest_send,
    rest_recv,
):
    times = lax.axis_size("tm")
    spaces = lax.axis_size("space")
    tme = lax.axis_index("tm")
    sme = lax.axis_index("space")
    own = layers * LAYER
    off = 2 * HALO
    end = off + layers
    around = [lax.rem(sme + spaces + step, spaces) for step in (1, -1, 2, -2)]
    heard = [sme >= 1, sme <= spaces - 2, sme >= 2, sme <= spaces - 3]
    sent = [heard[1], heard[0], heard[3], heard[2]]

    def start(copies):
        for slot, copy in copies:
            pl.when(sent[slot])(copy.start)

    def arrive(copies):
        for slot, copy in copies:
            pl.when(heard[slot])(copy.wait_recv)

    def finish_sends(copies):
        for slot, copy in copies:
            pl.when(sent[slot])(copy.wait_send)

    for slot in range(4):

        @pl.when(jnp.logical_not(heard[slot]))
        def _():
            tables_in[slot] = jnp.zeros(tables_in.shape[1:], F32)
            for point in range(times * count):
                piece_in[point, slot] = jnp.zeros(piece_in.shape[2:], F32)
                if slot < 2:
                    edge_in[point, slot] = jnp.zeros(edge_in.shape[2:], F32)
            for point in range(2):
                for turn in range(2):
                    if slot < 2:
                        block_in[point, turn, slot] = jnp.zeros(block_in.shape[3:], F32)
                        force_in[point, turn, slot] = jnp.zeros(force_in.shape[3:], F32)
                    else:
                        strip_in[point, turn, slot - 2] = jnp.zeros(strip_in.shape[3:], F32)


    pairs = (
        (ids_hbm, ids_ref),
        (walls_hbm, walls_ref),
        (scales_hbm, scales_ref),
        (guess_hbm, guess_ref),
        (faces_hbm, faces_ref),
        (volume_hbm, volume_ref),
        (init_hbm, init_ref),
        (forcing_hbm, forcing_ref),
    )
    loads = [pltpu.make_async_copy(a, b, load_sem.at[i]) for i, (a, b) in enumerate(pairs)]
    barrier = pltpu.get_barrier_semaphore()
    for slot in range(4):

        @pl.when(sent[slot])
        def _():
            pl.semaphore_signal(barrier, inc=1, device_id=(tme, around[slot]), device_id_type=MESH)

    for step in range(1, times):
        pl.semaphore_signal(
            barrier, inc=1, device_id=(lax.rem(tme + step, times), sme), device_id_type=MESH
        )

    for copy in loads:
        copy.start()

    def rows_of(layer, number=1):
        first = layer * LAYER
        if not isinstance(layer, int):
            first = pl.multiple_of(first, LAYER)
        return pl.ds(first, number * LAYER)

    for copy in loads[:3]:
        copy.wait()
    local = ids_ref[...].reshape(1, own) - sme * own
    tables_out[0:6, :] = (1 - walls_ref[...]).astype(F32)
    tables_out[6:7, :] = scales_ref[...].reshape(1, own)
    tables_out[7:8, :] = local.astype(F32)
    perm = one_hot(local, 0, own)
    perm_ref[...] = perm

    def permuted_pair(first, second):
        return doubled(select_rows_16(perm_ref[...], jnp.concatenate([first, second], axis=0)))

    loads[3].wait()
    one, two = permuted_pair(guess_ref[0], guess_ref[1])
    guess_grid[0] = one
    guess_grid[1] = two
    exts[1, rows_of(off, layers), :] = one

    def pack(target, source, first, number):
        for layer in range(number):
            target[layer * LAYER : (layer + 1) * LAYER, :] = jnp.where(
                left_lanes(LAYER),
                source[rows_of(first + layer), :],
                source[rows_of(first + number + layer), :],
            )

    def unpack(source, target, first, number):
        for layer in range(number):
            one, two = doubled(source[layer * LAYER : (layer + 1) * LAYER, :])
            target[rows_of(first + layer), :] = one
            target[rows_of(first + number + layer), :] = two

    half = HALO // 2

    def remote(source, target, send, recv, slot):
        return pltpu.make_async_remote_copy(
            src_ref=source,
            dst_ref=target,
            send_sem=send,
            recv_sem=recv,
            device_id=(tme, around[slot]),
            device_id_type=MESH,
        )

    def state_copies(point, turn):
        copies = [
            (side, remote(
                block_out.at[point, turn],
                block_in.at[point, turn, side],
                block_send.at[point, turn, side],
                block_recv.at[point, turn, side],
                side,
            ))
            for side in range(2)
        ]
        return copies + [
            (2 + side, remote(
                strip_out.at[point, turn, side],
                strip_in.at[point, turn, side],
                strip_send.at[point, turn, side],
                strip_recv.at[point, turn, side],
                2 + side,
            ))
            for side in range(2)
        ]

    def send_state(point, turn):
        ext = exts.at[point]
        pack(block_out.at[point, turn], ext, off, layers // 2)
        pack(strip_out.at[point, turn, 0], ext, end - 2, 1)
        pack(strip_out.at[point, turn, 1], ext, off, 1)
        start(state_copies(point, turn))

    def receive_state(point, turn):
        ext = exts.at[point]
        arrive(state_copies(point, turn))
        unpack(block_in.at[point, turn, 0], ext, off - layers, layers // 2)
        unpack(block_in.at[point, turn, 1], ext, end, layers // 2)
        unpack(strip_in.at[point, turn, 0], ext, off - layers - 2, 1)
        unpack(strip_in.at[point, turn, 1], ext, end + layers, 1)

    def force_copies(point, turn):
        return [
            (side, remote(
                force_out.at[point, turn, side],
                force_in.at[point, turn, side],
                force_send.at[point, turn, side],
                force_recv.at[point, turn, side],
                side,
            ))
            for side in range(2)
        ]

    def send_force(point, turn):
        source = sources.at[point, 2 * turn]
        pack(force_out.at[point, turn, 0], source, layers - HALO, half)
        pack(force_out.at[point, turn, 1], source, 0, half)
        start(force_copies(point, turn))

    def add_force(point, turn):
        ext = exts.at[point]
        arrive(force_copies(point, turn))
        for side, first in enumerate((off - HALO, end)):
            for layer in range(half):
                one, two = doubled(force_in[point, turn, side, layer * LAYER : (layer + 1) * LAYER, :])
                ext[rows_of(first + layer), :] = ext[rows_of(first + layer), :] + one
                ext[rows_of(first + half + layer), :] = ext[rows_of(first + half + layer), :] + two

    for copy in loads[4:7]:
        copy.wait()

    def permuted(field):
        return select_rows_16(perm_ref[...], jnp.concatenate([field, field], axis=0))

    @pl.when(tme == 0)
    def _():
        exts[0, rows_of(off, layers), :] = permuted(init_ref[...])

    pl.semaphore_wait(barrier, times - 1 + sum(here.astype(jnp.int32) for here in heard))

    guess_copy = pltpu.make_async_remote_copy(
        src_ref=guess_ref.at[count - 1],
        dst_ref=guess_in,
        send_sem=guess_send,
        recv_sem=guess_recv,
        device_id=(lax.rem(tme + 1, times), sme),
        device_id_type=MESH,
    )
    guess_copy.start()
    tables_copies = [
        (slot, remote(tables_out, tables_in.at[slot], tables_send.at[slot], tables_recv.at[slot], slot))
        for slot in range(4)
    ]
    start(tables_copies)

    @pl.when(tme == 0)
    def _():
        send_state(0, 0)

    send_state(1, 0)
    loads[7].wait()
    for step in (0, 2, 1, 3):
        one, two = permuted_pair(forcing_ref[step], forcing_ref[COARSEN + step])
        sources[0, step] = one
        sources[1, step] = two
        if step == 0:
            send_force(0, 0)
            send_force(1, 0)

    blocks = []
    for m in range(3):
        face = faces_ref[m]
        blocks.append(face.T)
        blocks.append(-face)
    blocks.append(volume_ref[...].T)
    blocks.append(jnp.zeros((DOF, DOF), F32))
    for pair in range(4):
        high, low = halves(jnp.concatenate(blocks[2 * pair : 2 * pair + 2], axis=1))
        weights[:, pair * 2 * DOF : (pair + 1) * 2 * DOF] = jnp.concatenate(
            [high, high, low, low], axis=0
        )

    def fill_table(first, number, hot, faces):
        flags, scale = table_of(hot, faces)
        table[rows_of(first, number), 0 : 6 * DOF] = flags
        table[rows_of(first, number), 6 * DOF : 8 * DOF] = scale

    fill_table(off - 1, layers, perm, tables_out[...])
    reach = 2 * HALO - 1 - layers
    spans = (
        (off - 1 - layers, 0, layers),
        (end - 1, 0, layers),
        (0, layers - reach, reach),
        (end - 1 + layers, 0, reach),
    )
    for slot, (place, begin, number) in enumerate(spans):
        arrive(tables_copies[slot : slot + 1])
        faces = tables_in[slot]
        hot = one_hot(faces[7:8].astype(jnp.int32), begin * LAYER, number * LAYER)
        fill_table(place, number, hot, faces)

    guess_copy.wait_recv()

    @pl.when(tme > 0)
    def _():
        exts[0, rows_of(off, layers), :] = permuted(guess_in[...])
        send_state(0, 0)

    send_force(1, 1)
    send_force(0, 1)

    def split_of(value):
        low = value - value.astype(BF16).astype(F32)
        return jnp.where(left_lanes(LAYER), value, low).astype(BF16)

    def products(blocks, part):
        rows = jnp.concatenate(blocks, axis=0)
        result = jnp.dot(
            jnp.concatenate([rows, rows], axis=1),
            weights[:, part * 4 * DOF : (part + 1) * 4 * DOF],
            preferred_element_type=F32,
        )
        return [result[i * LAYER : (i + 1) * LAYER] for i in range(len(blocks))]

    def combined(layer, flat, tall, below, above):
        left = left_lanes(LAYER)
        left3 = left.reshape(LAYER // GX, GX, 2 * DOF)
        px = flat[:, : 2 * DOF].reshape(LAYER // GX, GX, 2 * DOF)
        xs = jnp.where(left3, pltpu.roll(px, GX - 1, 1), pltpu.roll(px, 1, 1))
        py = flat[:, 2 * DOF :].reshape(LAYER // GX, GX, 2 * DOF)
        ys = jnp.where(
            left3,
            jnp.concatenate([py[1:], py[:1]], axis=0),
            jnp.concatenate([py[-1:], py[:-1]], axis=0),
        )
        zs = jnp.where(left, above[:, : 2 * DOF], below[:, : 2 * DOF])
        tab = slice((layer - 1) * LAYER, layer * LAYER)
        total = (
            table[tab, 0 : 2 * DOF] * xs.reshape(LAYER, 2 * DOF)
            + table[tab, 2 * DOF : 4 * DOF] * ys.reshape(LAYER, 2 * DOF)
        ) + (
            table[tab, 4 * DOF : 6 * DOF] * zs
            + table[tab, 6 * DOF : 8 * DOF] * tall[:, 2 * DOF :]
        )
        return total + swapped(total)

    def here(layer):
        return slice(layer * LAYER, (layer + 1) * LAYER)

    def advance(x, size, stage, layers_, flat, tall, finish):
        blocks = {}
        for layer in layers_:
            value = x[here(layer), :] + size / (4 - stage) * combined(
                layer, flat[layer], tall[layer], tall[layer - 1], tall[layer + 1]
            )
            if stage < 3:
                blocks[layer] = split_of(value)
            else:
                finish(layer, value)
        return blocks

    top = end + 2 * HALO

    def whole_step(x, size, low, high, finish, keep=False):
        blocks = {layer: split_of(x[here(layer), :]) for layer in range(low, high)}
        for stage in range(4):
            span = range(low + stage, high - stage)
            inner = span[1:-1]
            tall = dict(zip(span, products([blocks[layer] for layer in span], 1)))
            flat = dict(zip(inner, products([blocks[layer] for layer in inner], 0)))
            if keep:
                split[stage, 0] = blocks[span[0]]
                split[stage, 1] = blocks[span[-1]]
                for place, layer in enumerate((span[0], span[1], span[-1], span[-2])):
                    prod[stage, place] = tall[layer]
            blocks = advance(x, size, stage, inner, flat, tall, finish)

    def inner_step(x, size, finish, keep=True):
        whole_step(x, size, off - HALO, end + HALO, finish, keep)

    def outer_step(x, size, finish):
        blocks = {
            layer: split_of(x[here(layer), :])
            for layer in (*range(HALO), *range(top - HALO, top))
        }
        for stage in range(4):
            low, high = stage, top - stage - HALO
            span = (*range(low, low + HALO), *range(high, high + HALO))
            inner = (*range(low + 1, low + 1 + HALO), *range(high - 1, high - 1 + HALO))
            tall = dict(zip(span, products([blocks[layer] for layer in span], 1)))
            for place, layer in enumerate((low + HALO, low + HALO + 1, high - 1, high - 2)):
                tall[layer] = prod[stage, place]
            blocks[low + HALO] = split[stage, 0]
            blocks[high - 1] = split[stage, 1]
            flat = dict(zip(inner, products([blocks[layer] for layer in inner], 0)))
            blocks = advance(x, size, stage, inner, flat, tall, finish)

    core = lax.rem(sme, 2)
    far_first = core * (layers - HALO)
    rest_first = (1 - core) * HALO

    def residual_copies(index):
        point = count * tme + index
        result = []
        for step in range(times - 1, 0, -1):
            for source, target, send, recv in (
                (far_out, far_in, far_send, far_recv),
                (rest_out, rest_in, rest_send, rest_recv),
            ):
                result.append((
                    step,
                    pltpu.make_async_remote_copy(
                        src_ref=source.at[index],
                        dst_ref=target.at[point],
                        send_sem=send.at[index, step],
                        recv_sem=recv.at[point],
                        device_id=(lax.rem(tme + step, times), sme),
                        device_id_type=MESH,
                    ),
                ))
        return result

    final = count * tme + count - 1

    def edge_copies(point):
        return [
            (side, remote(
                edge_out.at[point, side],
                edge_in.at[point, side],
                edge_send.at[point, side],
                edge_recv.at[point, side],
                side,
            ))
            for side in range(2)
        ]

    def send_edge(point, side):
        pack(edge_out.at[point, side], errors.at[point], layers - HALO if side == 0 else 0, half)
        start(edge_copies(point)[side : side + 1])

    def landed(source, target, send, recv, point):
        pltpu.make_async_remote_copy(
            src_ref=source.at[0],
            dst_ref=target.at[point],
            send_sem=send.at[0, 0],
            recv_sem=recv.at[point],
            device_id=(lax.rem(tme + 1, times), sme),
            device_id_type=MESH,
        ).wait_recv()

    def piece_copies(point):
        return [
            (slot, remote(
                piece_out.at[point, (0, 1, 1, 0)[slot]],
                piece_in.at[point, slot],
                piece_send.at[point, slot],
                piece_recv.at[point, slot],
                slot,
            ))
            for slot in range(4)
        ]

    def send_pieces(point):
        pack(piece_out.at[point, 0], ext_a, off, 1)
        pack(piece_out.at[point, 1], ext_a, end - 2, 1)
        start(piece_copies(point))

    def receive_pieces(point):
        places = (off - layers, end + layers - 2, 0, end + layers)
        arrive(piece_copies(point))
        for slot in range(4):
            unpack(piece_in.at[point, slot], ext_a, places[slot], 1)

    def unpack_add(source, first):
        for layer in range(half):
            one, two = doubled(source[layer * LAYER : (layer + 1) * LAYER, :])
            low, high = rows_of(first + layer), rows_of(first + half + layer)
            ext_a[low, :] = ext_a[low, :] + one
            ext_a[high, :] = ext_a[high, :] + two

    def receive_edges(point, place):
        arrive(edge_copies(point))
        for side in range(2):
            place(side, edge_in.at[point, side])

    def pass_residual(point):
        passed = point < final
        foreign = point < count * tme

        @pl.when(jnp.logical_and(point <= final, foreign))
        def _():
            landed(far_out, far_in, far_send, far_recv, point)
            for side in range(2):

                @pl.when(jnp.logical_and(passed, core == 1 - side))
                def _():
                    start([(side, remote(
                        far_in.at[point],
                        edge_in.at[point, side],
                        edge_send.at[point, side],
                        edge_recv.at[point, side],
                        side,
                    ))])

            landed(rest_out, rest_in, rest_send, rest_recv, point)
            unpack(far_in.at[point], errors.at[point], far_first, half)
            unpack(rest_in.at[point], errors.at[point], rest_first, 1)
            for side in range(2):

                @pl.when(jnp.logical_and(passed, core == side))
                def _():
                    send_edge(point, side)

        @pl.when(jnp.logical_and(passed, jnp.logical_not(foreign)))
        def _():
            for side in range(2):
                send_edge(point, side)

    def begin_sweep():
        pass_residual(0)
        ext_a[rows_of(off, layers), :] = errors[0]

        @pl.when(final > 1)
        def _():
            send_pieces(0)

    def fine(index, carry):
        turn = index // 2
        point = lax.rem(index + jnp.minimum(tme, 1), 2)
        ext = exts.at[point]
        receive_state(point, turn)

        def finish(step):
            def store(layer, value):
                if off <= layer < end:
                    value = value + sources[point, 2 * turn + step, rows_of(layer - off), :]
                ext[rows_of(layer), :] = value

            return store

        whole_step(ext, 1.0, off - 2 * HALO, end + 2 * HALO, finish(0))
        add_force(point, turn)
        inner_step(ext, 1.0, finish(1), keep=False)

        @pl.when(turn == 0)
        def _():
            send_state(point, 1)

        @pl.when(turn == 1)
        def _():
            place = count * tme + point
            errors[place] = ext[rows_of(off, layers), :] - guess_grid[point]
            pack(far_out.at[point], errors.at[place], far_first, half)
            pack(rest_out.at[point], errors.at[place], rest_first, 1)
            for distance, copy in residual_copies(point):

                @pl.when(tme + distance < times)
                def _():
                    copy.start()

        return carry

    lax.fori_loop(0, 4, fine, 0)

    begin_sweep()
    pass_residual(1)

    receive_edges(0, lambda side, ref: unpack(ref, ext_a, off - HALO if side == 0 else end, half))

    def coarse(point, carry):
        def finish(layer, value):
            inside = rows_of(layer - off)
            value = value + errors[point, inside, :]
            ext_a[rows_of(layer), :] = value
            errors[point, inside, :] = value

        inner_step(ext_a, float(COARSEN), finish)

        @pl.when(point < final - 1)
        def _():
            send_pieces(point)

        @pl.when(point == 1)
        def _():
            pass_residual(2)

        @pl.when(point < final)
        def _():
            receive_pieces(point - 1)

            def finish_outer(layer, value):
                ext_a[rows_of(layer), :] = value

            outer_step(ext_a, float(COARSEN), finish_outer)
            receive_edges(
                point, lambda side, ref: unpack_add(ref, off - HALO if side == 0 else end)
            )

        pass_residual(point + 2)
        return carry

    lax.fori_loop(1, final + 1, coarse, 0)

    packed = jnp.where(left_lanes(own), errors[final - 1], errors[final])
    parts = lax.dot_general(
        jnp.concatenate(halves(packed), axis=1),
        perm_ref[...],
        (((0,), (0,)), ((), ())),
        preferred_element_type=F32,
    )
    result = parts[: 2 * DOF] + parts[2 * DOF :]
    out_ref[0] = result[:DOF]
    out_ref[1] = result[DOF:]

    guess_copy.wait_send()
    finish_sends(tables_copies)

    for point in range(2):
        for turn in range(2):
            finish_sends(state_copies(point, turn) + force_copies(point, turn))
    for index in range(2):
        for distance, copy in residual_copies(index):

            @pl.when(tme + distance < times)
            def _():
                copy.wait_send()

    def sweep_done(point, carry):
        finish_sends(edge_copies(point))

        @pl.when(point < final - 1)
        def _():
            finish_sends(piece_copies(point))

        return carry

    lax.fori_loop(0, final, sweep_done, 0)


def body(init_state, guess, forcing, volume_block, face_blocks, elem_scales, element_ids, neighbours, walls):
    own = element_ids.shape[0]
    layers = own // LAYER
    count = guess.shape[0]
    times = lax.axis_size("tm")
    points = times * count
    ext = (layers + 4 * HALO) * LAYER
    wide = 2 * DOF
    vmem = pltpu.VMEM
    dma = pltpu.SemaphoreType.DMA
    errors = pl.pallas_call(
        functools.partial(kernel, layers, count),
        out_shape=jax.ShapeDtypeStruct(guess.shape, F32),
        in_specs=[pl.BlockSpec(memory_space=pl.ANY)] * 8,
        out_specs=pl.BlockSpec(memory_space=pltpu.VMEM),
        scratch_shapes=[
            vmem(init_state.shape, F32),
            vmem(guess.shape, F32),
            vmem(forcing.shape, F32),
            vmem(volume_block.shape, F32),
            vmem(face_blocks.shape, F32),
            vmem((own,), F32),
            vmem((own,), jnp.int32),
            vmem(walls.shape, jnp.int32),
            vmem((4 * DOF, 8 * DOF), BF16),
            vmem((ext - 2 * LAYER, 8 * DOF), F32),
            vmem((own, own), BF16),
            vmem((2, COARSEN, own, wide), F32),
            vmem((2, own, wide), F32),
            vmem((2, ext, wide), F32),
            vmem((ext, wide), F32),
            vmem((4, 2, LAYER, wide), BF16),
            vmem((4, 4, LAYER, 4 * DOF), F32),
            vmem((points, own, wide), F32),
            vmem((8, own), F32),
            vmem((4, 8, own), F32),
            vmem((DOF, own), F32),
            vmem((2, 2, own // 2, wide), F32),
            vmem((2, 2, 2, own // 2, wide), F32),
            vmem((2, 2, 2, LAYER, wide), F32),
            vmem((2, 2, 2, LAYER, wide), F32),
            vmem((2, 2, 2, HALO // 2 * LAYER, wide), F32),
            vmem((2, 2, 2, HALO // 2 * LAYER, wide), F32),
            vmem((points, 2, LAYER, wide), F32),
            vmem((points, 4, LAYER, wide), F32),
            vmem((points, 2, HALO // 2 * LAYER, wide), F32),
            vmem((points, 2, HALO // 2 * LAYER, wide), F32),
            vmem((2, HALO // 2 * LAYER, wide), F32),
            vmem((points, HALO // 2 * LAYER, wide), F32),
            vmem((2, LAYER, wide), F32),
            vmem((points, LAYER, wide), F32),
            dma((8,)),
            dma((4,)),
            dma((4,)),
            dma,
            dma,
            dma((2, 2, 2)),
            dma((2, 2, 2)),
            dma((2, 2, 2)),
            dma((2, 2, 2)),
            dma((2, 2, 2)),
            dma((2, 2, 2)),
            dma((points, 4)),
            dma((points, 4)),
            dma((points, 2)),
            dma((points, 2)),
            dma((2, times)),
            dma((points,)),
            dma((2, times)),
            dma((points,)),
        ],
        compiler_params=pltpu.CompilerParams(
            collective_id=0, has_side_effects=True, vmem_limit_bytes=40 * 1024 * 1024
        ),
    )(
        *(
            pltpu.with_memory_space_constraint(field, pltpu.HBM)
            for field in (
                init_state,
                guess,
                forcing,
                volume_block,
                face_blocks,
                elem_scales,
                element_ids,
                walls,
            )
        )
    )
    return guess + errors


def solution(mesh):
    return jax.shard_map(
        body,
        mesh=mesh,
        in_specs=(
            P(None, "space"),
            P("tm", None, "space"),
            P("tm", None, "space"),
            P(),
            P(),
            P("space"),
            P("space"),
            P(None, "space"),
            P(None, "space"),
        ),
        out_specs=P("tm", None, "space"),
        check_vma=False,
    )
```

```python
import functools
import jax
import jax.numpy as jnp
from jax import lax
from jax.experimental import pallas as pl
from jax.experimental.pallas import tpu as pltpu
from jax.sharding import PartitionSpec as P

GX = 8
LAYER = 64
DOF = 64
COARSEN = 4
HALO = 4
MESH = pl.DeviceIdType.MESH
F32 = jnp.float32
BF16 = jnp.bfloat16


def halves(x):
    hi = x.astype(BF16)
    return hi, (x - hi.astype(F32)).astype(BF16)


def thirds(x):
    hi = x.astype(BF16)
    rest = x - hi.astype(F32)
    mid = rest.astype(BF16)
    return hi, mid, (rest - mid.astype(F32)).astype(BF16)


def times_t(a, b):
    return lax.dot_general(a, b, (((1,), (1,)), ((), ())), preferred_element_type=F32)


def select_rows(perm, values):
    hi, mid, lo = thirds(values)
    return (times_t(perm, hi) + times_t(perm, mid)) + times_t(perm, lo)


def left_lanes(rows):
    return lax.broadcasted_iota(jnp.int32, (rows, 2 * DOF), 1) < DOF


def swapped(x):
    return pltpu.roll(x, DOF, 1)


def doubled(packed):
    left = left_lanes(packed.shape[0])
    other = swapped(packed)
    return jnp.where(left, packed, other), jnp.where(left, other, packed)


def one_hot(ids_row, first, rows):
    cells = lax.broadcasted_iota(jnp.int32, (rows, ids_row.shape[1]), 0) + first
    return (ids_row == cells).astype(F32).astype(BF16)


def table_of(perm, faces):
    flags = jnp.concatenate(
        [jnp.broadcast_to(faces[f : f + 1], (DOF, faces.shape[1])) for f in range(6)], axis=0
    )
    scale = jnp.broadcast_to(faces[6:7], (2 * DOF, faces.shape[1]))
    return times_t(perm, flags.astype(BF16)), select_rows(perm, scale)


def kernel(
    layers,
    count,
    init_hbm,
    guess_hbm,
    forcing_hbm,
    volume_hbm,
    faces_hbm,
    scales_hbm,
    ids_hbm,
    walls_hbm,
    out_ref,
    init_ref,
    guess_ref,
    forcing_ref,
    volume_ref,
    faces_ref,
    scales_ref,
    ids_ref,
    walls_ref,
    weights,
    table,
    perm_ref,
    sources,
    guess_grid,
    exts,
    ext_a,
    spare,
    split,
    prod,
    errors,
    tables_out,
    tables_in,
    guess_in,
    block_out,
    block_in,
    strip_out,
    strip_in,
    force_out,
    force_in,
    piece_out,
    piece_in,
    edge_out,
    edge_in,
    far_out,
    far_in,
    rest_out,
    rest_in,
    load_sem,
    tables_send,
    tables_recv,
    guess_send,
    guess_recv,
    block_send,
    block_recv,
    strip_send,
    strip_recv,
    force_send,
    force_recv,
    piece_send,
    piece_recv,
    edge_send,
    edge_recv,
    far_send,
    far_recv,
    rest_send,
    rest_recv,
):
    times = lax.axis_size("tm")
    spaces = lax.axis_size("space")
    tme = lax.axis_index("tm")
    sme = lax.axis_index("space")
    own = layers * LAYER
    off = 2 * HALO
    end = off + layers
    around = [lax.rem(sme + spaces + step, spaces) for step in (1, -1, 2, -2)]
    heard = [sme >= 1, sme <= spaces - 2, sme >= 2, sme <= spaces - 3]
    sent = [heard[1], heard[0], heard[3], heard[2]]

    def start(copies):
        for slot, copy in copies:
            pl.when(sent[slot])(copy.start)

    def arrive(copies):
        for slot, copy in copies:
            pl.when(heard[slot])(copy.wait_recv)

    def finish_sends(copies):
        for slot, copy in copies:
            pl.when(sent[slot])(copy.wait_send)

    for slot in range(4):

        @pl.when(jnp.logical_not(heard[slot]))
        def _():
            tables_in[slot] = jnp.zeros(tables_in.shape[1:], F32)
            for point in range(times * count):
                piece_in[point, slot] = jnp.zeros(piece_in.shape[2:], F32)
                if slot < 2:
                    edge_in[point, slot] = jnp.zeros(edge_in.shape[2:], F32)
            for point in range(2):
                for turn in range(2):
                    if slot < 2:
                        block_in[point, turn, slot] = jnp.zeros(block_in.shape[3:], F32)
                        force_in[point, turn, slot] = jnp.zeros(force_in.shape[3:], F32)
                    else:
                        strip_in[point, turn, slot - 2] = jnp.zeros(strip_in.shape[3:], F32)


    pairs = (
        (ids_hbm, ids_ref),
        (walls_hbm, walls_ref),
        (scales_hbm, scales_ref),
        (guess_hbm, guess_ref),
        (faces_hbm, faces_ref),
        (volume_hbm, volume_ref),
        (init_hbm, init_ref),
        (forcing_hbm, forcing_ref),
    )
    loads = [pltpu.make_async_copy(a, b, load_sem.at[i]) for i, (a, b) in enumerate(pairs)]
    for copy in loads:
        copy.start()

    barrier = pltpu.get_barrier_semaphore()
    for slot in range(4):

        @pl.when(sent[slot])
        def _():
            pl.semaphore_signal(barrier, inc=1, device_id=(tme, around[slot]), device_id_type=MESH)

    for step in range(1, times):
        pl.semaphore_signal(
            barrier, inc=1, device_id=(lax.rem(tme + step, times), sme), device_id_type=MESH
        )

    def rows_of(layer, number=1):
        first = layer * LAYER
        if not isinstance(layer, int):
            first = pl.multiple_of(first, LAYER)
        return pl.ds(first, number * LAYER)

    for copy in loads[:3]:
        copy.wait()
    local = ids_ref[...].reshape(1, own) - sme * own
    tables_out[0:6, :] = (1 - walls_ref[...]).astype(F32)
    tables_out[6:7, :] = scales_ref[...].reshape(1, own)
    tables_out[7:8, :] = local.astype(F32)
    perm = one_hot(local, 0, own)
    perm_ref[...] = perm

    def permuted_pair(first, second):
        return doubled(select_rows(perm_ref[...], jnp.concatenate([first, second], axis=0)))

    loads[3].wait()
    one, two = permuted_pair(guess_ref[0], guess_ref[1])
    guess_grid[0] = one
    guess_grid[1] = two
    exts[1, rows_of(off, layers), :] = one

    def pack(target, source, first, number):
        for layer in range(number):
            target[layer * LAYER : (layer + 1) * LAYER, :] = jnp.where(
                left_lanes(LAYER),
                source[rows_of(first + layer), :],
                source[rows_of(first + number + layer), :],
            )

    def unpack(source, target, first, number):
        for layer in range(number):
            one, two = doubled(source[layer * LAYER : (layer + 1) * LAYER, :])
            target[rows_of(first + layer), :] = one
            target[rows_of(first + number + layer), :] = two

    half = HALO // 2

    def remote(source, target, send, recv, slot):
        return pltpu.make_async_remote_copy(
            src_ref=source,
            dst_ref=target,
            send_sem=send,
            recv_sem=recv,
            device_id=(tme, around[slot]),
            device_id_type=MESH,
        )

    def state_copies(point, turn):
        copies = [
            (side, remote(
                block_out.at[point, turn],
                block_in.at[point, turn, side],
                block_send.at[point, turn, side],
                block_recv.at[point, turn, side],
                side,
            ))
            for side in range(2)
        ]
        return copies + [
            (2 + side, remote(
                strip_out.at[point, turn, side],
                strip_in.at[point, turn, side],
                strip_send.at[point, turn, side],
                strip_recv.at[point, turn, side],
                2 + side,
            ))
            for side in range(2)
        ]

    def send_state(point, turn):
        ext = exts.at[point]
        copies = state_copies(point, turn)
        pack(block_out.at[point, turn], ext, off, layers // 2)
        start(copies[:2])
        pack(strip_out.at[point, turn, 0], ext, end - 2, 1)
        pack(strip_out.at[point, turn, 1], ext, off, 1)
        start(copies[2:])

    def receive_state(point, turn):
        ext = exts.at[point]
        copies = state_copies(point, turn)
        arrive(copies[:1])
        unpack(block_in.at[point, turn, 0], ext, off - layers, layers // 2)
        arrive(copies[1:2])
        unpack(block_in.at[point, turn, 1], ext, end, layers // 2)
        arrive(copies[2:])
        unpack(strip_in.at[point, turn, 0], ext, off - layers - 2, 1)
        unpack(strip_in.at[point, turn, 1], ext, end + layers, 1)

    def force_copies(point, turn):
        return [
            (side, remote(
                force_out.at[point, turn, side],
                force_in.at[point, turn, side],
                force_send.at[point, turn, side],
                force_recv.at[point, turn, side],
                side,
            ))
            for side in range(2)
        ]

    def send_force(point, turn):
        source = sources.at[point, 2 * turn]
        pack(force_out.at[point, turn, 0], source, layers - HALO, half)
        pack(force_out.at[point, turn, 1], source, 0, half)
        start(force_copies(point, turn))

    def add_force(point, turn):
        ext = exts.at[point]
        arrive(force_copies(point, turn))
        for side, first in enumerate((off - HALO, end)):
            for layer in range(half):
                one, two = doubled(force_in[point, turn, side, layer * LAYER : (layer + 1) * LAYER, :])
                ext[rows_of(first + layer), :] = ext[rows_of(first + layer), :] + one
                ext[rows_of(first + half + layer), :] = ext[rows_of(first + half + layer), :] + two

    for copy in loads[4:7]:
        copy.wait()

    @pl.when(tme == 0)
    def _():
        one, _ = permuted_pair(init_ref[...], init_ref[...])
        exts[0, rows_of(off, layers), :] = one

    pl.semaphore_wait(barrier, times - 1 + sum(here.astype(jnp.int32) for here in heard))

    guess_copy = pltpu.make_async_remote_copy(
        src_ref=guess_ref.at[count - 1],
        dst_ref=guess_in,
        send_sem=guess_send,
        recv_sem=guess_recv,
        device_id=(lax.rem(tme + 1, times), sme),
        device_id_type=MESH,
    )
    guess_copy.start()
    tables_copies = [
        (slot, remote(tables_out, tables_in.at[slot], tables_send.at[slot], tables_recv.at[slot], slot))
        for slot in range(4)
    ]
    start(tables_copies)

    @pl.when(tme == 0)
    def _():
        send_state(0, 0)

    send_state(1, 0)
    loads[7].wait()
    for step in (0, 2, 1, 3):
        one, two = permuted_pair(forcing_ref[step], forcing_ref[COARSEN + step])
        sources[0, step] = one
        sources[1, step] = two
        if step == 0:
            send_force(0, 0)
            send_force(1, 0)

    blocks = []
    for m in range(3):
        face = faces_ref[m]
        blocks.append(face.T)
        blocks.append(-face)
    blocks.append(volume_ref[...].T)
    blocks.append(jnp.zeros((DOF, DOF), F32))
    for pair in range(4):
        high, low = halves(jnp.concatenate(blocks[2 * pair : 2 * pair + 2], axis=1))
        weights[:, pair * 2 * DOF : (pair + 1) * 2 * DOF] = jnp.concatenate(
            [high, high, low, low], axis=0
        )

    def fill_table(first, number, hot, faces):
        flags, scale = table_of(hot, faces)
        table[rows_of(first, number), 0 : 6 * DOF] = flags
        table[rows_of(first, number), 6 * DOF : 8 * DOF] = scale

    fill_table(off - 1, layers, perm, tables_out[...])
    reach = 2 * HALO - 1 - layers
    spans = (
        (off - 1 - layers, 0, layers),
        (end - 1, 0, layers),
        (0, layers - reach, reach),
        (end - 1 + layers, 0, reach),
    )
    for slot, (place, begin, number) in enumerate(spans):
        arrive(tables_copies[slot : slot + 1])
        faces = tables_in[slot]
        hot = one_hot(faces[7:8].astype(jnp.int32), begin * LAYER, number * LAYER)
        fill_table(place, number, hot, faces)

    guess_copy.wait_recv()

    @pl.when(tme > 0)
    def _():
        one, _ = permuted_pair(guess_in[...], guess_in[...])
        exts[0, rows_of(off, layers), :] = one
        send_state(0, 0)

    send_force(1, 1)
    send_force(0, 1)

    def split_of(value):
        low = value - value.astype(BF16).astype(F32)
        return jnp.where(left_lanes(LAYER), value, low).astype(BF16)

    def products(blocks, part):
        rows = jnp.concatenate(blocks, axis=0)
        result = jnp.dot(
            jnp.concatenate([rows, rows], axis=1),
            weights[:, part * 4 * DOF : (part + 1) * 4 * DOF],
            preferred_element_type=F32,
        )
        return [result[i * LAYER : (i + 1) * LAYER] for i in range(len(blocks))]

    def combined(layer, flat, tall, below, above):
        left = left_lanes(LAYER)
        left3 = left.reshape(LAYER // GX, GX, 2 * DOF)
        px = flat[:, : 2 * DOF].reshape(LAYER // GX, GX, 2 * DOF)
        xs = jnp.where(left3, pltpu.roll(px, GX - 1, 1), pltpu.roll(px, 1, 1))
        py = flat[:, 2 * DOF :].reshape(LAYER // GX, GX, 2 * DOF)
        ys = jnp.where(
            left3,
            jnp.concatenate([py[1:], py[:1]], axis=0),
            jnp.concatenate([py[-1:], py[:-1]], axis=0),
        )
        zs = jnp.where(left, above[:, : 2 * DOF], below[:, : 2 * DOF])
        tab = slice((layer - 1) * LAYER, layer * LAYER)
        total = (
            table[tab, 0 : 2 * DOF] * xs.reshape(LAYER, 2 * DOF)
            + table[tab, 2 * DOF : 4 * DOF] * ys.reshape(LAYER, 2 * DOF)
        ) + (
            table[tab, 4 * DOF : 6 * DOF] * zs
            + table[tab, 6 * DOF : 8 * DOF] * tall[:, 2 * DOF :]
        )
        return total + swapped(total)

    def here(layer):
        return slice(layer * LAYER, (layer + 1) * LAYER)

    def advance(x, size, stage, layers_, flat, tall, finish):
        blocks = {}
        for layer in layers_:
            value = x[here(layer), :] + size / (4 - stage) * combined(
                layer, flat[layer], tall[layer], tall[layer - 1], tall[layer + 1]
            )
            if stage < 3:
                blocks[layer] = split_of(value)
            else:
                finish(layer, value)
        return blocks

    top = end + 2 * HALO

    def whole_step(x, size, low, high, finish, keep=False):
        blocks = {layer: split_of(x[here(layer), :]) for layer in range(low, high)}
        for stage in range(4):
            span = range(low + stage, high - stage)
            inner = span[1:-1]
            tall = dict(zip(span, products([blocks[layer] for layer in span], 1)))
            flat = dict(zip(inner, products([blocks[layer] for layer in inner], 0)))
            if keep:
                split[stage, 0] = blocks[span[0]]
                split[stage, 1] = blocks[span[-1]]
                for place, layer in enumerate((span[0], span[1], span[-1], span[-2])):
                    prod[stage, place] = tall[layer]
            blocks = advance(x, size, stage, inner, flat, tall, finish)

    def inner_step(x, size, finish, keep=True):
        whole_step(x, size, off - HALO, end + HALO, finish, keep)

    def outer_step(x, size, finish):
        blocks = {
            layer: split_of(x[here(layer), :])
            for layer in (*range(HALO), *range(top - HALO, top))
        }
        for stage in range(4):
            low, high = stage, top - stage - HALO
            span = (*range(low, low + HALO), *range(high, high + HALO))
            inner = (*range(low + 1, low + 1 + HALO), *range(high - 1, high - 1 + HALO))
            tall = dict(zip(span, products([blocks[layer] for layer in span], 1)))
            for place, layer in enumerate((low + HALO, low + HALO + 1, high - 1, high - 2)):
                tall[layer] = prod[stage, place]
            blocks[low + HALO] = split[stage, 0]
            blocks[high - 1] = split[stage, 1]
            flat = dict(zip(inner, products([blocks[layer] for layer in inner], 0)))
            blocks = advance(x, size, stage, inner, flat, tall, finish)

    core = lax.rem(sme, 2)
    far_first = core * (layers - HALO)
    rest_first = (1 - core) * HALO

    def residual_copies(index):
        point = count * tme + index
        result = []
        for step in range(times - 1, 0, -1):
            for source, target, send, recv in (
                (far_out, far_in, far_send, far_recv),
                (rest_out, rest_in, rest_send, rest_recv),
            ):
                result.append((
                    step,
                    pltpu.make_async_remote_copy(
                        src_ref=source.at[index],
                        dst_ref=target.at[point],
                        send_sem=send.at[index, step],
                        recv_sem=recv.at[point],
                        device_id=(lax.rem(tme + step, times), sme),
                        device_id_type=MESH,
                    ),
                ))
        return result

    final = count * tme + count - 1

    def edge_copies(point):
        return [
            (side, remote(
                edge_out.at[point, side],
                edge_in.at[point, side],
                edge_send.at[point, side],
                edge_recv.at[point, side],
                side,
            ))
            for side in range(2)
        ]

    def send_edge(point, side):
        pack(edge_out.at[point, side], errors.at[point], layers - HALO if side == 0 else 0, half)
        start(edge_copies(point)[side : side + 1])

    def landed(source, target, send, recv, point):
        pltpu.make_async_remote_copy(
            src_ref=source.at[0],
            dst_ref=target.at[point],
            send_sem=send.at[0, 0],
            recv_sem=recv.at[point],
            device_id=(lax.rem(tme + 1, times), sme),
            device_id_type=MESH,
        ).wait_recv()

    def piece_copies(point):
        return [
            (slot, remote(
                piece_out.at[point, (0, 1, 1, 0)[slot]],
                piece_in.at[point, slot],
                piece_send.at[point, slot],
                piece_recv.at[point, slot],
                slot,
            ))
            for slot in range(4)
        ]

    def send_pieces(point):
        copies = piece_copies(point)
        pack(piece_out.at[point, 1], ext_a, end - 2, 1)
        start(copies[1:3])
        pack(piece_out.at[point, 0], ext_a, off, 1)
        start([copies[0], copies[3]])

    def receive_pieces(point):
        places = (off - layers, end + layers - 2, 0, end + layers)
        arrive(piece_copies(point))
        for slot in range(4):
            unpack(piece_in.at[point, slot], ext_a, places[slot], 1)

    def receive_edges(point, place):
        arrive(edge_copies(point))
        for side in range(2):
            place(side, edge_in.at[point, side])

    def pass_residual(point):
        passed = point < final
        foreign = point < count * tme

        @pl.when(jnp.logical_and(point <= final, foreign))
        def _():
            landed(far_out, far_in, far_send, far_recv, point)
            for side in range(2):

                @pl.when(jnp.logical_and(passed, core == 1 - side))
                def _():
                    start([(side, remote(
                        far_in.at[point],
                        edge_in.at[point, side],
                        edge_send.at[point, side],
                        edge_recv.at[point, side],
                        side,
                    ))])

            landed(rest_out, rest_in, rest_send, rest_recv, point)
            unpack(far_in.at[point], errors.at[point], far_first, half)
            unpack(rest_in.at[point], errors.at[point], rest_first, 1)
            for side in range(2):

                @pl.when(jnp.logical_and(passed, core == side))
                def _():
                    send_edge(point, side)

        @pl.when(jnp.logical_and(passed, jnp.logical_not(foreign)))
        def _():
            for side in range(2):
                send_edge(point, side)

    def begin_sweep():
        pass_residual(0)
        ext_a[rows_of(off, layers), :] = errors[0]

        @pl.when(final > 1)
        def _():
            send_pieces(0)

    def fine(index, carry):
        @pl.when(jnp.logical_and(index == 3, tme == times - 1))
        def _():
            begin_sweep()

        turn = index // 2
        point = lax.rem(index + jnp.minimum(tme, 1), 2)
        ext = exts.at[point]
        receive_state(point, turn)

        def finish(step):
            def store(layer, value):
                if off <= layer < end:
                    value = value + sources[point, 2 * turn + step, rows_of(layer - off), :]
                ext[rows_of(layer), :] = value

            return store

        whole_step(ext, 1.0, off - 2 * HALO, end + 2 * HALO, finish(0))
        add_force(point, turn)
        inner_step(ext, 1.0, finish(1), keep=False)

        @pl.when(turn == 0)
        def _():
            send_state(point, 1)

        @pl.when(turn == 1)
        def _():
            place = count * tme + point
            errors[place] = ext[rows_of(off, layers), :] - guess_grid[point]
            pack(far_out.at[point], errors.at[place], far_first, half)
            pack(rest_out.at[point], errors.at[place], rest_first, 1)
            for distance, copy in residual_copies(point):

                @pl.when(tme + distance < times)
                def _():
                    copy.start()

        return carry

    lax.fori_loop(0, 4, fine, 0)

    @pl.when(tme < times - 1)
    def _():
        begin_sweep()

    pass_residual(1)

    receive_edges(0, lambda side, ref: unpack(ref, ext_a, off - HALO if side == 0 else end, half))

    def coarse(point, carry):
        def finish(layer, value):
            inside = rows_of(layer - off)
            value = value + errors[point, inside, :]
            ext_a[rows_of(layer), :] = value
            errors[point, inside, :] = value

        inner_step(ext_a, float(COARSEN), finish)

        @pl.when(point < final - 1)
        def _():
            send_pieces(point)

        @pl.when(point == 1)
        def _():
            pass_residual(2)

        pass_residual(point + 2)

        @pl.when(point < final)
        def _():
            receive_edges(
                point, lambda side, ref: unpack(ref, spare, off - HALO if side == 0 else end, half)
            )
            receive_pieces(point - 1)

            def finish_outer(layer, value):
                ext_a[rows_of(layer), :] = value + spare[rows_of(layer), :]

            outer_step(ext_a, float(COARSEN), finish_outer)

        return carry

    lax.fori_loop(1, final + 1, coarse, 0)

    packed = jnp.where(left_lanes(own), errors[final - 1], errors[final])
    parts = [
        lax.dot_general(part, perm_ref[...], (((0,), (0,)), ((), ())), preferred_element_type=F32)
        for part in halves(packed)
    ]
    result = parts[0] + parts[1]
    out_ref[0] = result[:DOF]
    out_ref[1] = result[DOF:]

    guess_copy.wait_send()
    finish_sends(tables_copies)

    for point in range(2):
        for turn in range(2):
            finish_sends(state_copies(point, turn) + force_copies(point, turn))
    for index in range(2):
        for distance, copy in residual_copies(index):

            @pl.when(tme + distance < times)
            def _():
                copy.wait_send()

    def sweep_done(point, carry):
        finish_sends(edge_copies(point))

        @pl.when(point < final - 1)
        def _():
            finish_sends(piece_copies(point))

        return carry

    lax.fori_loop(0, final, sweep_done, 0)


def body(init_state, guess, forcing, volume_block, face_blocks, elem_scales, element_ids, neighbours, walls):
    own = element_ids.shape[0]
    layers = own // LAYER
    count = guess.shape[0]
    times = lax.axis_size("tm")
    points = times * count
    ext = (layers + 4 * HALO) * LAYER
    wide = 2 * DOF
    vmem = pltpu.VMEM
    dma = pltpu.SemaphoreType.DMA
    errors = pl.pallas_call(
        functools.partial(kernel, layers, count),
        out_shape=jax.ShapeDtypeStruct(guess.shape, F32),
        in_specs=[pl.BlockSpec(memory_space=pl.ANY)] * 8,
        out_specs=pl.BlockSpec(memory_space=pltpu.VMEM),
        scratch_shapes=[
            vmem(init_state.shape, F32),
            vmem(guess.shape, F32),
            vmem(forcing.shape, F32),
            vmem(volume_block.shape, F32),
            vmem(face_blocks.shape, F32),
            vmem((own,), F32),
            vmem((own,), jnp.int32),
            vmem(walls.shape, jnp.int32),
            vmem((4 * DOF, 8 * DOF), BF16),
            vmem((ext - 2 * LAYER, 8 * DOF), F32),
            vmem((own, own), BF16),
            vmem((2, COARSEN, own, wide), F32),
            vmem((2, own, wide), F32),
            vmem((2, ext, wide), F32),
            vmem((ext, wide), F32),
            vmem((ext, wide), F32),
            vmem((4, 2, LAYER, wide), BF16),
            vmem((4, 4, LAYER, 4 * DOF), F32),
            vmem((points, own, wide), F32),
            vmem((8, own), F32),
            vmem((4, 8, own), F32),
            vmem((DOF, own), F32),
            vmem((2, 2, own // 2, wide), F32),
            vmem((2, 2, 2, own // 2, wide), F32),
            vmem((2, 2, 2, LAYER, wide), F32),
            vmem((2, 2, 2, LAYER, wide), F32),
            vmem((2, 2, 2, HALO // 2 * LAYER, wide), F32),
            vmem((2, 2, 2, HALO // 2 * LAYER, wide), F32),
            vmem((points, 2, LAYER, wide), F32),
            vmem((points, 4, LAYER, wide), F32),
            vmem((points, 2, HALO // 2 * LAYER, wide), F32),
            vmem((points, 2, HALO // 2 * LAYER, wide), F32),
            vmem((2, HALO // 2 * LAYER, wide), F32),
            vmem((points, HALO // 2 * LAYER, wide), F32),
            vmem((2, LAYER, wide), F32),
            vmem((points, LAYER, wide), F32),
            dma((8,)),
            dma((4,)),
            dma((4,)),
            dma,
            dma,
            dma((2, 2, 2)),
            dma((2, 2, 2)),
            dma((2, 2, 2)),
            dma((2, 2, 2)),
            dma((2, 2, 2)),
            dma((2, 2, 2)),
            dma((points, 4)),
            dma((points, 4)),
            dma((points, 2)),
            dma((points, 2)),
            dma((2, times)),
            dma((points,)),
            dma((2, times)),
            dma((points,)),
        ],
        compiler_params=pltpu.CompilerParams(
            collective_id=0, has_side_effects=True, vmem_limit_bytes=40 * 1024 * 1024
        ),
    )(
        *(
            pltpu.with_memory_space_constraint(field, pltpu.HBM)
            for field in (
                init_state,
                guess,
                forcing,
                volume_block,
                face_blocks,
                elem_scales,
                element_ids,
                walls,
            )
        )
    )
    return guess + errors


def solution(mesh):
    return jax.shard_map(
        body,
        mesh=mesh,
        in_specs=(
            P(None, "space"),
            P("tm", None, "space"),
            P("tm", None, "space"),
            P(),
            P(),
            P("space"),
            P("space"),
            P(None, "space"),
            P(None, "space"),
        ),
        out_specs=P("tm", None, "space"),
        check_vma=False,
    )
```
